32 devices in a mesh: dp: 8 (over z, y), unit: 4 (over x, core).
Axes of the slice: x: 2, y: 2, z: 4, core: 2. Of those that a mesh axis runs over, the one named last changes fastest.
Arguments:
- layer_input: bfloat16 [32768, 768], P(('dp', 'unit')), may hold values from -18 to 18
- teacher: bfloat16 [32768, 768], P(('dp', 'unit')), may hold values from -18 to 18
- cotangent: bfloat16 [32768, 768], P(('dp', 'unit')), may hold values from -6 to 6
- key_valid: int32 [32768], P(('dp', 'unit')), may hold values 0 or 1
- seg_lengths: int32 [32, 3], P(('dp', 'unit')), may hold values from 1 to 512, 1024 in all within a row
- head_mask: int32 [12], replicated, may hold values from 0 to 1, as said below
- hidden_mask: int32 [768], replicated, may hold values 0 or 1
- inter_mask: int32 [3072], replicated, may hold values 0 or 1
- proj_master: float32 [768, 3840], P(('dp', 'unit')), may hold values from -0.649519 to 0.649519
- proj_first: float32 [768, 3840], P(('dp', 'unit')), may hold values from -0.00061035156 to 0.00061035156
- proj_second: float32 [768, 3840], P(('dp', 'unit')), may hold values from 6.5123705e-11 to 1.0419793e-09
- up_master: float32 [768, 3072], P('dp', 'unit'), may hold values from -0.21875 to 0.21875
- up_first: float32 [768, 3072], P('dp', 'unit'), may hold values from -0.00061035156 to 0.00061035156
- up_second: float32 [768, 3072], P('dp', 'unit'), may hold values from 6.5123705e-11 to 1.0419793e-09
- down_master: float32 [3072, 768], P('unit', 'dp'), may hold values from -0.21875 to 0.21875
- down_first: float32 [3072, 768], P('unit', 'dp'), may hold values from -0.00061035156 to 0.00061035156
- down_second: float32 [3072, 768], P('unit', 'dp'), may hold values from 6.5123705e-11 to 1.0419793e-09
- vector_master: float32 [13, 768], replicated, may hold values from -1 to 2.5
- vector_first: float32 [13, 768], replicated, may hold values from -0.00061035156 to 0.00061035156
- vector_second: float32 [13, 768], replicated, may hold values from 6.5123705e-11 to 1.0419793e-09
Outputs:
- layer_out: bfloat16 [32768, 768], P(('dp', 'unit'))
- input_grad: float32 [32768, 768], P(('dp', 'unit'))
- grad_norm: float32 [], replicated
- distill_loss: float32 [], replicated
- proj_master_new: float32 [768, 3840], P(('dp', 'unit'))
- proj_first_new: float32 [768, 3840], P(('dp', 'unit'))
- proj_second_new: float32 [768, 3840], P(('dp', 'unit'))
- up_master_new: float32 [768, 3072], P('dp', 'unit')
- up_first_new: float32 [768, 3072], P('dp', 'unit')
- up_second_new: float32 [768, 3072], P('dp', 'unit')
- down_master_new: float32 [3072, 768], P('unit', 'dp')
- down_first_new: float32 [3072, 768], P('unit', 'dp')
- down_second_new: float32 [3072, 768], P('unit', 'dp')
- vector_master_new: float32 [13, 768], replicated
- vector_first_new: float32 [13, 768], replicated
- vector_second_new: float32 [13, 768], replicated
The draws below stay inside these ranges and needn't reach their ends.
Inputs may be any that keep to these rules, and one draw needn't show every extreme that they name: `seg_lengths`: each row holds the lengths of the 3 sequences that fill one pack of 1024 consecutive tokens, in order. `head_mask`: exactly one head is pruned (0), all others are 1.
All inputs are finite; a program needn't handle non-finite values. No bound on the sum of `key_valid` on one device may be relied on, other than what follows from the above.
Results may differ from the reference program's by a relative error of at most 0.017.
Values may be sent and summed in bfloat16 or wider, within the bound.
No kernel may reach another device: no remote copies, remote signals or barrier semaphores. Data moves between devices by JAX's collectives and lax.ppermute only.
A program may use at most 192 MiB of HBM per device.

```python
import math
from functools import partial
import jax
import jax.numpy as jnp
import numpy as np
from jax import lax

D = 768
H = 12
HD = 64
FF = 3072
SEQ_BLOCK = 1024
NSEG = 3
STEP = 10
TOKENS = 32768


def draw_layer_input(key, part):
    key = jax.random.fold_in(key, 11)
    place = jnp.arange(D, dtype=jnp.float32) / (D - 1)
    base = jnp.clip(jax.random.normal(key, (TOKENS, D), jnp.float32), -6.0, 6.0)
    return (base * jnp.exp(place * math.log(3.0))[None, :]).astype(jnp.bfloat16)


def draw_teacher(key, part):
    key = jax.random.fold_in(key, 23)
    place = jnp.arange(TOKENS, dtype=jnp.float32) / (TOKENS - 1)
    base = jnp.clip(jax.random.normal(key, (TOKENS, D), jnp.float32), -6.0, 6.0)
    return (base * (1.0 + 2.0 * place)[:, None]).astype(jnp.bfloat16)


def draw_head_mask(key, part):
    key = jax.random.fold_in(key, 53)
    pruned = jax.random.randint(key, (), 0, H, dtype=jnp.int32)
    return (jnp.arange(H, dtype=jnp.int32) != pruned).astype(jnp.int32)


def draw_proj_master(key, part):
    key = jax.random.fold_in(key, 37)
    base = jnp.clip(jax.random.normal(key, (D, 5 * D), jnp.float32), -6.0, 6.0)
    block = jnp.arange(5 * D, dtype=jnp.int32) // D
    scale = jnp.where(block < 2, 0.6, jnp.where(block == 3, 3.0, 1.0))
    return base * scale[None, :] / math.sqrt(D)


def draw_vector_master(key, part):
    key = jax.random.fold_in(key, 41)
    rows = 9 + FF // D
    noise = jnp.clip(jax.random.normal(key, (rows, D), jnp.float32), -3.0, 3.0)
    place = jnp.arange(D, dtype=jnp.float32) / (D - 1)
    index = jnp.arange(rows, dtype=jnp.int32)[:, None]
    is_gain = (index == 3) | (index == 6)
    gains = (0.6 + 1.2 * place)[None, :] * (1.0 + 0.1 * noise)
    return jnp.where(is_gain, gains, 0.3 * noise)


def place_ends(result, key, least, top_value):
    spot = [jax.random.randint(jax.random.fold_in(key, axis), (), 0, length) for axis, length in enumerate(result.shape)]
    widest = result.shape.index(max(result.shape))
    beside = spot[:widest] + [(spot[widest] + 1) % result.shape[widest]] + spot[widest + 1:]
    return result.at[tuple(spot)].set(least).at[tuple(beside)].set(top_value)


def steps_of(stream_key, shape, split, low, top_value):
    def one(dim, blocks):
        steps = jax.random.uniform(jax.random.fold_in(jax.random.fold_in(stream_key, 6), dim), (blocks,), jnp.float32, low / len(split), top_value / len(split))
        return jnp.repeat(jnp.exp(steps), shape[dim] // blocks).reshape((-1,) + (1,) * (len(shape) - dim - 1))

    level = one(*split[0])
    for cut in split[1:]:
        level = level * one(*cut)
    return level


def profile(count, total, reach, lean):
    portions = [(1 << 20) // math.isqrt(grade ** lean) + 1 for grade in range(2, count + 1)]
    surplus, holding = total - reach - (count - 1), [1] * (count - 1)
    while surplus > 0:
        free = [i for i in range(count - 1) if holding[i] < reach]
        mass, remaining = sum([portions[i] for i in free]), surplus
        for i in free:
            more = min(reach - holding[i], max(1, remaining * portions[i] // mass), surplus)
            holding[i] = holding[i] + more
            surplus = surplus - more
    return np.array([reach] + holding)


def uneven_parts(own_key, number_of, total, bound, slope):
    if number_of == 2:
        one = jax.random.randint(own_key, (), max(1, total - bound), min(bound, total - 1) + 1)
        return jnp.stack([one, total - one])
    sizes = jnp.asarray(profile(number_of, total, bound, slope), jnp.int32)
    couples = (number_of - 1) // 2
    source_of, taker = sizes[1:1 + 2 * couples:2], sizes[2:2 + 2 * couples:2]
    room = jnp.minimum(source_of - 1, bound - taker)
    passed = jax.random.randint(jax.random.fold_in(own_key, 1), (couples,), 0, 1 << 20) % (room + 1)
    sizes = sizes.at[1:1 + 2 * couples:2].set(source_of - passed).at[2:2 + 2 * couples:2].set(taker + passed)
    return sizes[jax.random.permutation(jax.random.fold_in(own_key, 2), number_of)]


def bell_draw(key, dims, scale, most, pieces=(), kind=jnp.bfloat16):
    level = steps_of(key, dims, pieces, -0.22, 0.18) if pieces else 1.0
    drawn = jax.random.normal(key, dims, jnp.float32) * scale * level
    return jnp.minimum(jnp.maximum(drawn, -most), most).astype(kind)


def setup_inputs(seed: int = 0) -> dict:
    splits = jax.random.split(jax.random.key(seed), 21)
    layer_input = draw_layer_input(jax.random.fold_in(splits[20], 71), 0)
    teacher = draw_teacher(jax.random.fold_in(splits[20], 71), 0)
    cotangent = bell_draw(splits[2], (TOKENS, D), 1.0, 6.0, ((0, 32),))
    key_valid = place_ends((jax.random.randint(splits[3], (TOKENS,), 0, 8) < 7).astype(jnp.int32), jax.random.fold_in(splits[3], 1), 0, 1)
    seg_lengths = jax.vmap(lambda own: uneven_parts(own, NSEG, SEQ_BLOCK, SEQ_BLOCK // 2, 0))(jax.random.split(splits[4], (TOKENS // SEQ_BLOCK))).reshape((TOKENS // SEQ_BLOCK, NSEG)).astype(jnp.int32)
    head_mask = draw_head_mask(jax.random.fold_in(splits[20], 71), 0)
    hidden_mask = place_ends((jax.random.randint(splits[6], (D,), 0, 8) < 7).astype(jnp.int32), jax.random.fold_in(splits[6], 1), 0, 1)
    inter_mask = place_ends((jax.random.randint(splits[7], (FF,), 0, 4) < 3).astype(jnp.int32), jax.random.fold_in(splits[7], 1), 0, 1)
    proj_master = draw_proj_master(jax.random.fold_in(splits[20], 71), 0)
    proj_first = bell_draw(splits[9], (D, 5 * D), (0.111 / (5 * D * D + 2 * D * FF + 13 * D) ** 0.5), 0.00061035156, ((0, 32),), jnp.float32)
    proj_second = jnp.clip(jnp.exp(math.log(1.0419792806359851e-09) - 2.7725887 * jax.random.uniform(splits[10], (D, 5 * D), jnp.float32) ** steps_of(splits[10], (D, 5 * D), ((0, 32),), -0.2, 0.2)), 6.512370503974907e-11, 1.0419792806359851e-09)
    up_master = bell_draw(splits[11], (D, FF), D ** -0.5, 0.21875, ((0, 8), (1, 4)), jnp.float32)
    up_first = bell_draw(splits[12], (D, FF), (0.111 / (5 * D * D + 2 * D * FF + 13 * D) ** 0.5), 0.00061035156, ((0, 8), (1, 4)), jnp.float32)
    up_second = jnp.clip(jnp.exp(math.log(1.0419792806359851e-09) - 2.7725887 * jax.random.uniform(splits[13], (D, FF), jnp.float32) ** steps_of(splits[13], (D, FF), ((0, 8), (1, 4)), -0.2, 0.2)), 6.512370503974907e-11, 1.0419792806359851e-09)
    down_master = bell_draw(splits[14], (FF, D), (FF // 4) ** -0.5, 0.21875, ((0, 4), (1, 8)), jnp.float32)
    down_first = bell_draw(splits[15], (FF, D), (0.111 / (5 * D * D + 2 * D * FF + 13 * D) ** 0.5), 0.00061035156, ((0, 4), (1, 8)), jnp.float32)
    down_second = jnp.clip(jnp.exp(math.log(1.0419792806359851e-09) - 2.7725887 * jax.random.uniform(splits[16], (FF, D), jnp.float32) ** steps_of(splits[16], (FF, D), ((0, 4), (1, 8)), -0.2, 0.2)), 6.512370503974907e-11, 1.0419792806359851e-09)
    vector_master = draw_vector_master(jax.random.fold_in(splits[20], 71), 0)
    vector_first = bell_draw(splits[18], (9 + FF // D, D), (0.111 / (5 * D * D + 2 * D * FF + 13 * D) ** 0.5), 0.00061035156, (), jnp.float32)
    vector_second = jnp.clip(jnp.exp(jax.random.uniform(splits[19], (9 + FF // D, D), jnp.float32, math.log(6.512370503974907e-11), math.log(1.0419792806359851e-09))), 6.512370503974907e-11, 1.0419792806359851e-09)
    return dict(layer_input=layer_input, teacher=teacher, cotangent=cotangent, key_valid=key_valid, seg_lengths=seg_lengths, head_mask=head_mask, hidden_mask=hidden_mask, inter_mask=inter_mask, proj_master=proj_master, proj_first=proj_first, proj_second=proj_second, up_master=up_master, up_first=up_first, up_second=up_second, down_master=down_master, down_first=down_first, down_second=down_second, vector_master=vector_master, vector_first=vector_first, vector_second=vector_second)


EPS_NORM = 1e-05
BETA_ONE = 0.9
BETA_TWO = 0.999
ADAM_EPS = 1e-08
RATE_MATRIX = 0.1
RATE_VECTOR = 1.0
DECAY_MATRIX = 0.01
CLIP_NORM = 1.0
MASKED = -1000000000.0
HIGH = lax.Precision.HIGHEST

@jax.custom_vjp
def low(v):
    return lax.optimization_barrier(v.astype(jnp.bfloat16)).astype(jnp.float32)

@jax.custom_vjp
def low_back(v):
    return v

def low_keep(v):
    return (low(v), None)

def low_pass(kept, grad):
    return (grad,)

def back_keep(v):
    return (v, None)

def back_low(kept, grad):
    return (low(grad),)
low.defvjp(low_keep, low_pass)
low_back.defvjp(back_keep, back_low)

def layer_norm(value, gain, shift):
    mean = lax.optimization_barrier(jnp.mean(value, axis=-1, keepdims=True))
    centred = value - mean
    spread = lax.optimization_barrier(jnp.mean(centred * centred, axis=-1, keepdims=True))
    return centred * lax.rsqrt(spread + EPS_NORM) * gain + shift

def segment_ids(lengths, count):
    ends = jnp.cumsum(lengths)
    places = jnp.arange(count, dtype=jnp.int32)
    return lax.optimization_barrier(jnp.sum((places[:, None] >= ends[None, :-1]).astype(jnp.int32), axis=1))

def pack_attention(packed):
    query, keys, values, segment, valid = packed
    scores = jnp.einsum('qhd,khd->hqk', query, keys, precision=HIGH) * HD ** (-0.5)
    scores = low_back(scores)
    places = jnp.arange(query.shape[0], dtype=jnp.int32)
    allowed = (segment[:, None] == segment[None, :]) & ((valid[None, :] > 0.5) | (places[:, None] == places[None, :]))
    scores = jnp.where(allowed[None], scores, MASKED)
    probs = low(jax.nn.softmax(scores, axis=-1))
    return jnp.einsum('hqk,khd->qhd', probs, values, precision=HIGH)

def group_forward(proj, up_weight, down_weight, vectors, inputs, target, segments, valid, gates):
    head_gate, hidden_gate, unit_gate = gates
    w_qkv = low(proj[:, :3 * D])
    w_out = low(proj[:, 3 * D:4 * D])
    w_dist = low(proj[:, 4 * D:])
    count = inputs.shape[0]
    packs = count // SEQ_BLOCK
    bias_qkv = jnp.concatenate([vectors[0], jnp.zeros((D,), jnp.float32), vectors[1]])
    qkv = low_back(low(jnp.dot(inputs, w_qkv, precision=HIGH) + bias_qkv))
    qkv = qkv.reshape(packs, SEQ_BLOCK, 3, H, HD)
    context = lax.map(jax.checkpoint(pack_attention), (qkv[:, :, 0], qkv[:, :, 1], qkv[:, :, 2], segments, valid.reshape(packs, SEQ_BLOCK)))
    context = context.reshape(count, H, HD) * head_gate[None, :, None]
    context = low_back(low(context.reshape(count, D)))
    attn = low_back(jnp.dot(context, w_out, precision=HIGH) + vectors[2]) * hidden_gate
    first = layer_norm(inputs + attn, vectors[3], vectors[4])
    inner = low_back(jnp.dot(low(first), low(up_weight), precision=HIGH) + vectors[9:].reshape(FF))
    active = low(jax.nn.gelu(inner, approximate=False) * unit_gate)
    branch = low_back(jnp.dot(active, low(down_weight), precision=HIGH) + vectors[5]) * hidden_gate
    out = layer_norm(first + branch, vectors[6], vectors[7])
    student = low_back(jnp.dot(low(out), w_dist, precision=HIGH) + vectors[8])
    error = student - target
    half_sq = 0.5 * jnp.sum(valid[:, None] * error * error)
    return (out, half_sq)

def adamw(master, first, second, grad, rate, decay):
    first_new = BETA_ONE * first + (1.0 - BETA_ONE) * grad
    second_new = BETA_TWO * second + (1.0 - BETA_TWO) * grad * grad
    first_hat = first_new / (1.0 - BETA_ONE ** STEP)
    second_hat = second_new / (1.0 - BETA_TWO ** STEP)
    master_new = master - rate * (first_hat / (jnp.sqrt(second_hat) + ADAM_EPS) + decay * master)
    return (master_new, first_new, second_new)

def reference(layer_input, teacher, cotangent, key_valid, seg_lengths, head_mask, hidden_mask, inter_mask, proj_master, proj_first, proj_second, up_master, up_first, up_second, down_master, down_first, down_second, vector_master, vector_first, vector_second):
    group = 4 * SEQ_BLOCK
    groups = TOKENS // group
    segments = jax.vmap(partial(segment_ids, count=SEQ_BLOCK))(seg_lengths)
    gates = (head_mask.astype(jnp.float32), hidden_mask.astype(jnp.float32), inter_mask.astype(jnp.float32))
    stacked = (layer_input.astype(jnp.float32).reshape(groups, group, D), teacher.astype(jnp.float32).reshape(groups, group, D), cotangent.astype(jnp.float32).reshape(groups, group, D), key_valid.astype(jnp.float32).reshape(groups, group), segments.reshape(groups, group // SEQ_BLOCK, SEQ_BLOCK))

    def one_group(carry, packed):
        inputs, target, upstream, valid, segs = packed

        def forward(proj, up_weight, down_weight, vectors, values):
            return group_forward(proj, up_weight, down_weight, vectors, values, target, segs, valid, gates)
        (out, half_sq), pullback = jax.vjp(forward, proj_master, up_master, down_master, vector_master, inputs)
        grads = pullback((upstream, jnp.ones((), jnp.float32)))
        carry = (carry[0] + grads[0], carry[1] + grads[1], carry[2] + grads[2], carry[3] + grads[3], carry[4] + half_sq)
        return (carry, (out.astype(jnp.bfloat16), grads[4]))
    start = (jnp.zeros_like(proj_master), jnp.zeros_like(up_master), jnp.zeros_like(down_master), jnp.zeros_like(vector_master), jnp.zeros((), jnp.float32))
    totals, (outs, input_grads) = lax.scan(one_group, start, stacked)
    g_proj, g_up, g_down, g_vec, half_total = totals
    squares = jnp.sum(g_proj * g_proj) + jnp.sum(g_up * g_up) + jnp.sum(g_down * g_down) + jnp.sum(g_vec * g_vec)
    grad_norm = jnp.sqrt(squares)
    clip = jnp.minimum(1.0, CLIP_NORM / (grad_norm + 1e-06))
    proj_new = adamw(proj_master, proj_first, proj_second, clip * g_proj, RATE_MATRIX, DECAY_MATRIX)
    up_new = adamw(up_master, up_first, up_second, clip * g_up, RATE_MATRIX, DECAY_MATRIX)
    down_new = adamw(down_master, down_first, down_second, clip * g_down, RATE_MATRIX, DECAY_MATRIX)
    vector_new = adamw(vector_master, vector_first, vector_second, clip * g_vec, RATE_VECTOR, 0.0)
    distill_loss = 2.0 * half_total / (TOKENS * D)
    return (outs.reshape(TOKENS, D), input_grads.reshape(TOKENS, D), grad_norm, distill_loss, proj_new[0], proj_new[1], proj_new[2], up_new[0], up_new[1], up_new[2], down_new[0], down_new[1], down_new[2], vector_new[0], vector_new[1], vector_new[2])
```

```python
import jax
import jax.numpy as jnp
from jax import lax
from jax.experimental import pallas as pl
from jax.experimental.pallas import tpu as pltpu
from jax.sharding import PartitionSpec as P

STEP = 10
EPS_NORM = 1e-05
BETA_ONE = 0.9
BETA_TWO = 0.999
ADAM_EPS = 1e-08
RATE_MATRIX = 0.1
RATE_VECTOR = 1.0
DECAY_MATRIX = 0.01
CLIP_NORM = 1.0
HEAD = 64
LANES = 128
QUERY_ROWS = 256
MASKED = -1e30
AXES = ("dp", "unit")
f32 = jnp.float32
bf16 = jnp.bfloat16


def dot(left, right):
    return jnp.dot(left, right, preferred_element_type=f32)


def dot_rows(left, right):
    return lax.dot_general(left, right, (((0,), (0,)), ((), ())), preferred_element_type=f32)


def dot_cols(left, right):
    return lax.dot_general(left, right, (((1,), (1,)), ((), ())), preferred_element_type=f32)


def build_bias(bias_ref, valid_ref, end_one, end_two):
    count = bias_ref.shape[0]
    for start in range(0, count, QUERY_ROWS):
        key = lax.broadcasted_iota(jnp.int32, (count, QUERY_ROWS), 0)
        query = lax.broadcasted_iota(jnp.int32, (count, QUERY_ROWS), 1) + start
        seg_key = (key >= end_one).astype(jnp.int32) + (key >= end_two).astype(jnp.int32)
        seg_query = (query >= end_one).astype(jnp.int32) + (query >= end_two).astype(jnp.int32)
        allowed = (seg_key == seg_query) & ((valid_ref[...] > 0) | (key == query))
        bias_ref[:, start : start + QUERY_ROWS] = jnp.where(allowed, 0.0, MASKED)


def over_window(first_row, end_one, end_two, count, body):
    low = jnp.where(first_row < end_one, 0, jnp.where(first_row < end_two, end_one, end_two))
    last_row = first_row + QUERY_ROWS - 1
    high = jnp.where(last_row < end_one, end_one, jnp.where(last_row < end_two, end_two, count))
    low = (low // 16) * 16
    done = jnp.bool_(False)
    for width in [w for w in (272, 528, 784) if w < count] + [count]:
        start = jnp.minimum(low, count - width)
        fits = (high - start) <= width
        run = fits & jnp.logical_not(done)

        @pl.when(run)
        def _(width=width, start=start):
            body(width, pl.multiple_of(start, 16))

        done = done | fits


def pair_position(heads_ref):
    step = pl.program_id(0)
    head = heads_ref[step]
    fresh = (step == 0) | (heads_ref[jnp.maximum(step - 1, 0)] // 2 != head // 2)
    lane = lax.broadcasted_iota(jnp.int32, (1, LANES), 1)
    return fresh, (lane // HEAD) == (head % 2)


def forward_kernel(
    heads_ref, ends_ref, q_ref, k_ref, v_ref, valid_ref, ctx_ref, lse_ref, bias_ref, qm_ref
):
    count = q_ref.shape[0]
    end_one, end_two = ends_ref[0], ends_ref[1]
    fresh, keep = pair_position(heads_ref)

    @pl.when(pl.program_id(0) == 0)
    def _():
        build_bias(bias_ref, valid_ref, end_one, end_two)

    @pl.when(fresh)
    def _():
        ctx_ref[...] = jnp.zeros_like(ctx_ref)

    qm_ref[...] = jnp.where(keep, q_ref[...] * bf16(HEAD**-0.5), bf16(0))

    def step(index, carry):
        first_row = pl.multiple_of(index * QUERY_ROWS, QUERY_ROWS)
        queries = pl.ds(first_row, QUERY_ROWS)

        def body(width, start):
            window = pl.ds(start, width)
            scores = dot_cols(k_ref[window, :], qm_ref[queries, :]) + bias_ref[window, queries]
            peak = jnp.max(scores, axis=0, keepdims=True)
            expo = jnp.exp(scores - peak)
            total = jnp.sum(expo, axis=0, keepdims=True)
            out = (dot_rows(v_ref[window, :], expo.astype(bf16)) * (1.0 / total)).T
            ctx_ref[queries, :] = jnp.where(keep, out.astype(bf16), ctx_ref[queries, :])
            lse_ref[0, :, queries] = peak + jnp.log(total)

        over_window(first_row, end_one, end_two, count, body)
        return carry

    lax.fori_loop(0, count // QUERY_ROWS, step, 0)


def pair_block(count, offset):
    return pl.BlockSpec((count, LANES), lambda i, heads, ends: (0, heads[i] // 2 + offset))


def attention_forward(qkv, valid_column, ends, heads, all_heads):
    count, width = qkv.shape[0], qkv.shape[1] // 3
    active, pairs = heads.shape[0], width // LANES
    return pl.pallas_call(
        forward_kernel,
        grid_spec=pltpu.PrefetchScalarGridSpec(
            num_scalar_prefetch=2,
            grid=(active,),
            in_specs=[
                pair_block(count, 0),
                pair_block(count, pairs),
                pair_block(count, 2 * pairs),
                pl.BlockSpec((count, 1), lambda i, heads, ends: (0, 0)),
            ],
            out_specs=[
                pair_block(count, 0),
                pl.BlockSpec((1, 1, count), lambda i, heads, ends: (heads[i], 0, 0)),
            ],
            scratch_shapes=[pltpu.VMEM((count, count), f32), pltpu.VMEM((count, LANES), bf16)],
        ),
        out_shape=[
            jax.ShapeDtypeStruct((count, width), bf16),
            jax.ShapeDtypeStruct((all_heads, 1, count), f32),
        ],
        compiler_params=pltpu.CompilerParams(vmem_limit_bytes=40 * 2**20),
        cost_estimate=pl.CostEstimate(
            flops=30 * count * count * HEAD * active,
            bytes_accessed=8 * count * width,
            transcendentals=count * count * active,
        ),
        name="attention_forward",
    )(heads, ends, qkv, qkv, qkv, valid_column)


def backward_kernel(
    heads_ref, ends_ref, q_ref, k_ref, v_ref, do_ref, ctx_ref, lse_ref, valid_ref,
    dq_ref, dk_ref, dv_ref, sums_ref,
    bias_ref, qm_ref, dom_ref, dk_total, dv_total, delta_ref,
):
    count = q_ref.shape[0]
    end_one, end_two = ends_ref[0], ends_ref[1]
    fresh, keep = pair_position(heads_ref)

    @pl.when(pl.program_id(0) == 0)
    def _():
        build_bias(bias_ref, valid_ref, end_one, end_two)

    @pl.when(fresh)
    def _():
        dq_ref[...] = jnp.zeros_like(dq_ref)
        dk_total[...] = jnp.zeros_like(dk_total)
        dv_total[...] = jnp.zeros_like(dv_total)

    qm_ref[...] = jnp.where(keep, q_ref[...] * bf16(HEAD**-0.5), bf16(0))
    dom_ref[...] = jnp.where(keep, do_ref[...], bf16(0))
    product = dom_ref[...].astype(f32) * ctx_ref[...].astype(f32)
    delta_ref[...] = jnp.sum(product.T, axis=0, keepdims=True)

    def step(index, carry):
        first_row = pl.multiple_of(index * QUERY_ROWS, QUERY_ROWS)
        queries = pl.ds(first_row, QUERY_ROWS)

        def body(width, start):
            window = pl.ds(start, width)
            keys, query, grad = k_ref[window, :], qm_ref[queries, :], dom_ref[queries, :]
            scores = dot_cols(keys, query) + bias_ref[window, queries]
            probs = jnp.exp(scores - lse_ref[0, :, queries])
            d_probs = dot_cols(v_ref[window, :], grad)
            d_scores = (probs * (d_probs - delta_ref[:, queries])).astype(bf16)
            dv_total[window, :] += dot(probs.astype(bf16), grad)
            dk_total[window, :] += dot(d_scores, query)
            d_query = (dot_rows(keys, d_scores) * HEAD**-0.5).T
            dq_ref[queries, :] = jnp.where(keep, d_query.astype(bf16), dq_ref[queries, :])

        over_window(first_row, end_one, end_two, count, body)
        return carry

    lax.fori_loop(0, count // QUERY_ROWS, step, 0)
    dk_ref[...] = dk_total[...].astype(bf16)
    d_value = dv_total[...].astype(bf16)
    dv_ref[...] = d_value
    sums_ref[0:1, :] = jnp.sum(dq_ref[...].astype(f32), axis=0, keepdims=True)
    sums_ref[1:2, :] = jnp.sum(d_value.astype(f32), axis=0, keepdims=True)


def attention_backward(qkv, d_ctx, ctx, lse, valid_column, ends, heads):
    count, width = ctx.shape
    active, pairs = heads.shape[0], width // LANES
    part = jax.ShapeDtypeStruct((count, width), bf16)
    return pl.pallas_call(
        backward_kernel,
        grid_spec=pltpu.PrefetchScalarGridSpec(
            num_scalar_prefetch=2,
            grid=(active,),
            in_specs=[
                pair_block(count, 0),
                pair_block(count, pairs),
                pair_block(count, 2 * pairs),
                pair_block(count, 0),
                pair_block(count, 0),
                pl.BlockSpec((1, 1, count), lambda i, heads, ends: (heads[i], 0, 0)),
                pl.BlockSpec((count, 1), lambda i, heads, ends: (0, 0)),
            ],
            out_specs=[pair_block(count, 0)] * 3
            + [pl.BlockSpec((8, LANES), lambda i, heads, ends: (0, heads[i] // 2))],
            scratch_shapes=[
                pltpu.VMEM((count, count), f32),
                pltpu.VMEM((count, LANES), bf16),
                pltpu.VMEM((count, LANES), bf16),
                pltpu.VMEM((count, LANES), f32),
                pltpu.VMEM((count, LANES), f32),
                pltpu.VMEM((1, count), f32),
            ],
        ),
        out_shape=[part, part, part, jax.ShapeDtypeStruct((8, width), f32)],
        compiler_params=pltpu.CompilerParams(vmem_limit_bytes=40 * 2**20),
        cost_estimate=pl.CostEstimate(
            flops=30 * count * count * HEAD * active,
            bytes_accessed=16 * count * width,
            transcendentals=count * count * active,
        ),
        name="attention_backward",
    )(heads, ends, qkv, qkv, qkv, d_ctx, ctx, lse, valid_column)


def normalize(value):
    mean = jnp.mean(value, axis=-1, keepdims=True)
    centred = value - mean
    root = lax.rsqrt(jnp.mean(centred * centred, axis=-1, keepdims=True) + EPS_NORM)
    return centred * root, root


def normalize_back(grad, hat, root, gain):
    scaled = grad * gain
    mean_one = jnp.mean(scaled, axis=-1, keepdims=True)
    mean_two = jnp.mean(scaled * hat, axis=-1, keepdims=True)
    back = root * (scaled - mean_one - hat * mean_two)
    return back, jnp.sum(grad * hat, axis=0), jnp.sum(grad, axis=0)


def adamw(master, first, second, grad, rate, decay):
    first_new = BETA_ONE * first + (1.0 - BETA_ONE) * grad
    second_new = BETA_TWO * second + (1.0 - BETA_TWO) * grad * grad
    first_hat = first_new / (1.0 - BETA_ONE**STEP)
    second_hat = second_new / (1.0 - BETA_TWO**STEP)
    master_new = master - rate * (first_hat / (jnp.sqrt(second_hat) + ADAM_EPS) + decay * master)
    return master_new, first_new, second_new


def gather_rows(shard):
    return lax.all_gather(shard, AXES, axis=0, tiled=True)


def scatter_rows(grad):
    return lax.psum_scatter(grad.astype(bf16), AXES, scatter_dimension=0, tiled=True).astype(f32)


def gather_tiles(shard):
    tiles = lax.all_gather(shard, AXES, axis=0)
    dp, unit = lax.axis_size("dp"), lax.axis_size("unit")
    tiles = tiles.reshape(dp, unit, *shard.shape).transpose(0, 2, 1, 3)
    return tiles.reshape(dp * shard.shape[0], unit * shard.shape[1])


def scatter_tiles(grad):
    dp, unit = lax.axis_size("dp"), lax.axis_size("unit")
    rows, cols = grad.shape[0] // dp, grad.shape[1] // unit
    tiles = grad.astype(bf16).reshape(dp, rows, unit, cols).transpose(0, 2, 1, 3)
    tiles = tiles.reshape(dp * unit * rows, cols)
    return lax.psum_scatter(tiles, AXES, scatter_dimension=0, tiled=True).astype(f32)


def shards(
    layer_input, teacher, cotangent, key_valid, seg_lengths, head_mask, hidden_mask, inter_mask,
    proj_master, proj_first, proj_second, up_master, up_first, up_second,
    down_master, down_first, down_second, vector_master, vector_first, vector_second,
):
    rows, width = layer_input.shape
    all_heads = head_mask.shape[0]
    hidden_gate = hidden_mask.astype(f32)
    unit_gate = inter_mask.astype(f32)
    valid = key_valid.astype(f32)[:, None]
    valid_column = key_valid[:, None]
    ends = jnp.cumsum(seg_lengths[0])
    pruned = jnp.argmin(head_mask).astype(jnp.int32)
    heads = jnp.arange(all_heads - 1, dtype=jnp.int32)
    heads = heads + (heads >= pruned).astype(jnp.int32)
    head_gate = jnp.repeat(head_mask.astype(bf16), HEAD)
    vec = vector_master
    inner_bias = vec[9:].reshape(-1)

    proj_low = proj_master.astype(bf16)
    w_qkv = gather_rows(proj_low[:, : 3 * width])
    w_rest = gather_rows(proj_low[:, 3 * width :])
    w_out, w_dist = w_rest[:, :width], w_rest[:, width:]
    w_up = gather_tiles(up_master.astype(bf16))
    w_down = gather_tiles(down_master.astype(bf16).T)

    bias_qkv = jnp.concatenate([vec[0], jnp.zeros_like(vec[0]), vec[1]])
    qkv = (dot(layer_input, w_qkv) + bias_qkv).astype(bf16)
    ctx, lse = attention_forward(qkv, valid_column, ends, heads, all_heads)
    attn = (dot(ctx, w_out) + vec[2]) * hidden_gate
    hat_one, root_one = normalize(layer_input.astype(f32) + attn)
    first = hat_one * vec[3] + vec[4]
    first_low = first.astype(bf16)

    inner = dot(first_low, w_up) + inner_bias
    cdf = 0.5 * (1.0 + lax.erf(inner * 0.7071067811865476))
    pdf = jnp.exp(-0.5 * inner * inner) * 0.3989422804014327
    active = (inner * cdf * unit_gate).astype(bf16)
    slope = ((cdf + inner * pdf) * unit_gate).astype(bf16)
    branch = (dot_cols(active, w_down) + vec[5]) * hidden_gate
    hat_two, root_two = normalize(first + branch)
    out_low = (hat_two * vec[6] + vec[7]).astype(bf16)
    error = dot(out_low, w_dist) + vec[8] - teacher.astype(f32)
    half_sq = 0.5 * jnp.sum(valid * error * error)
    d_student = (valid * error).astype(bf16)
    g_dist = dot_rows(out_low, d_student)
    g_bias_dist = jnp.sum(d_student.astype(f32), axis=0)
    d_out = cotangent.astype(f32) + dot_cols(d_student, w_dist)
    d_second, g_gain_two, g_shift_two = normalize_back(d_out, hat_two, root_two, vec[6])
    d_branch = (d_second * hidden_gate).astype(bf16)
    g_bias_two = jnp.sum(d_branch.astype(f32), axis=0)

    d_inner = (dot(d_branch, w_down) * slope.astype(f32)).astype(bf16)
    g_down = scatter_tiles(dot_rows(d_branch, active))
    g_up = scatter_tiles(dot_rows(first_low, d_inner))
    g_inner_bias = jnp.sum(d_inner.astype(f32), axis=0)
    d_first = d_second + dot_cols(d_inner, w_up)
    d_first_sum, g_gain_one, g_shift_one = normalize_back(d_first, hat_one, root_one, vec[3])
    d_attn = (d_first_sum * hidden_gate).astype(bf16)
    g_bias_out = jnp.sum(d_attn.astype(f32), axis=0)
    g_out = dot_rows(ctx, d_attn)
    g_rest = scatter_rows(jnp.concatenate([g_out, g_dist], axis=1))
    d_ctx = dot_cols(d_attn, w_out).astype(bf16) * head_gate
    dq, dk, dv, bias_sums = attention_backward(qkv, d_ctx, ctx, lse, valid_column, ends, heads)
    d_qkv = jnp.concatenate([dq, dk, dv], axis=1)
    g_qkv = scatter_rows(dot_rows(layer_input, d_qkv))
    input_grad = d_first_sum + dot_cols(d_qkv, w_qkv)

    g_proj = jnp.concatenate([g_qkv, g_rest], axis=1)
    vector_grad = jnp.concatenate(
        [
            jnp.stack(
                [
                    bias_sums[0], bias_sums[1], g_bias_out, g_gain_one, g_shift_one,
                    g_bias_two, g_gain_two, g_shift_two, g_bias_dist,
                ]
            ),
            g_inner_bias.reshape(-1, width),
        ]
    )
    shard_sq = jnp.sum(g_proj * g_proj) + jnp.sum(g_up * g_up) + jnp.sum(g_down * g_down)
    vector_grad, half_total, shard_total = lax.psum((vector_grad, half_sq, shard_sq), AXES)
    grad_norm = jnp.sqrt(shard_total + jnp.sum(vector_grad * vector_grad))
    clip = jnp.minimum(1.0, CLIP_NORM / (grad_norm + 1e-06))
    all_tokens = rows * lax.axis_size("dp") * lax.axis_size("unit")
    distill_loss = 2.0 * half_total / (all_tokens * width)
    return (
        out_low,
        input_grad,
        grad_norm,
        distill_loss,
        *adamw(proj_master, proj_first, proj_second, clip * g_proj, RATE_MATRIX, DECAY_MATRIX),
        *adamw(up_master, up_first, up_second, clip * g_up, RATE_MATRIX, DECAY_MATRIX),
        *adamw(down_master, down_first, down_second, clip * g_down.T, RATE_MATRIX, DECAY_MATRIX),
        *adamw(vector_master, vector_first, vector_second, clip * vector_grad, RATE_VECTOR, 0.0),
    )


def solution(mesh):
    by_token = P(AXES, None)
    tile, tile_back = P("dp", "unit"), P("unit", "dp")
    in_specs = (
        (by_token, by_token, by_token, P(AXES), by_token, P(), P(), P())
        + (by_token,) * 3
        + (tile,) * 3
        + (tile_back,) * 3
        + (P(),) * 3
    )
    out_specs = (
        (by_token, by_token, P(), P()) + (by_token,) * 3 + (tile,) * 3 + (tile_back,) * 3 + (P(),) * 3
    )
    return jax.shard_map(shards, mesh=mesh, in_specs=in_specs, out_specs=out_specs, check_vma=False)
```

```python
from functools import partial

import jax
import jax.numpy as jnp
from jax import lax
from jax.experimental import pallas as pl
from jax.experimental.pallas import tpu as pltpu
from jax.sharding import PartitionSpec as P

STEP = 10
EPS_NORM = 1e-05
BETA_ONE = 0.9
BETA_TWO = 0.999
ADAM_EPS = 1e-08
RATE_MATRIX = 0.1
RATE_VECTOR = 1.0
DECAY_MATRIX = 0.01
CLIP_NORM = 1.0
HEAD = 64
LANES = 128
HEADS_PER_CHUNK = 4
QUERY_ROWS = 256
MASKED = -1e30
AXES = ("dp", "unit")
f32 = jnp.float32
bf16 = jnp.bfloat16


def dot(left, right):
    return jnp.dot(left, right, preferred_element_type=f32)


def dot_rows(left, right):
    return lax.dot_general(left, right, (((0,), (0,)), ((), ())), preferred_element_type=f32)


def dot_cols(left, right):
    return lax.dot_general(left, right, (((1,), (1,)), ((), ())), preferred_element_type=f32)


def build_bias(bias_ref, valid_ref, end_one, end_two):
    count = bias_ref.shape[0]
    for start in range(0, count, QUERY_ROWS):
        key = lax.broadcasted_iota(jnp.int32, (count, QUERY_ROWS), 0)
        query = lax.broadcasted_iota(jnp.int32, (count, QUERY_ROWS), 1) + start
        seg_key = (key >= end_one).astype(jnp.int32) + (key >= end_two).astype(jnp.int32)
        seg_query = (query >= end_one).astype(jnp.int32) + (query >= end_two).astype(jnp.int32)
        allowed = (seg_key == seg_query) & ((valid_ref[...] > 0) | (key == query))
        bias_ref[:, start : start + QUERY_ROWS] = jnp.where(allowed, 0.0, MASKED)


def over_window(first_row, end_one, end_two, count, body):
    low = jnp.where(first_row < end_one, 0, jnp.where(first_row < end_two, end_one, end_two))
    last_row = first_row + QUERY_ROWS - 1
    high = jnp.where(last_row < end_one, end_one, jnp.where(last_row < end_two, end_two, count))
    low = (low // 16) * 16
    done = jnp.bool_(False)
    for width in [w for w in (272, 528, 784) if w < count] + [count]:
        start = jnp.minimum(low, count - width)
        fits = (high - start) <= width
        run = fits & jnp.logical_not(done)

        @pl.when(run)
        def _(width=width, start=start):
            body(width, pl.multiple_of(start, 16))

        done = done | fits


def lanes_of(head):
    lane = lax.broadcasted_iota(jnp.int32, (1, LANES), 1)
    return (lane // HEAD) == (head % 2)


def forward_kernel(
    chunk, gate_ref, ends_ref, q_ref, k_ref, v_ref, valid_ref, *refs
):
    ctx_ref, lse_ref, bias_ref, qm_ref = refs[-4:]
    count = q_ref.shape[0]
    end_one, end_two = ends_ref[0], ends_ref[1]
    head = pl.program_id(0)
    keep = lanes_of(head)

    @pl.when(head == 0)
    def _():
        build_bias(bias_ref, valid_ref, end_one, end_two)

    @pl.when(head % 2 == 0)
    def _():
        ctx_ref[...] = jnp.zeros_like(ctx_ref)

    def step(index, carry):
        first_row = pl.multiple_of(index * QUERY_ROWS, QUERY_ROWS)
        queries = pl.ds(first_row, QUERY_ROWS)

        def body(width, start):
            window = pl.ds(start, width)
            scores = dot_cols(k_ref[window, :], qm_ref[queries, :]) + bias_ref[window, queries]
            peak = jnp.max(scores, axis=0, keepdims=True)
            expo = jnp.exp(scores - peak)
            total = jnp.sum(expo, axis=0, keepdims=True)
            out = (dot_rows(v_ref[window, :], expo.astype(bf16)) * (1.0 / total)).T
            ctx_ref[queries, :] = jnp.where(keep, out.astype(bf16), ctx_ref[queries, :])
            lse_ref[0, :, queries] = peak + jnp.log(total)

        over_window(first_row, end_one, end_two, count, body)
        return carry

    @pl.when(gate_ref[chunk * HEADS_PER_CHUNK + head] > 0)
    def _():
        qm_ref[...] = jnp.where(keep, q_ref[...] * bf16(HEAD**-0.5), bf16(0))
        lax.fori_loop(0, count // QUERY_ROWS, step, 0)


def pair_block(count, offset):
    return pl.BlockSpec((count, LANES), lambda i, gate, ends: (0, i // 2 + offset))


def attention_forward(chunk, qkv, valid_column, ends, gate, ctx_before, width):
    count, pairs = qkv.shape[0], HEADS_PER_CHUNK // 2
    in_specs = [
        pair_block(count, 0),
        pair_block(count, pairs),
        pair_block(count, 2 * pairs),
        pl.BlockSpec((count, 1), lambda i, gate, ends: (0, 0)),
    ]
    operands = [gate, ends, qkv, qkv, qkv, valid_column]
    aliases = {}
    if ctx_before is not None:
        in_specs.append(pl.BlockSpec(memory_space=pl.ANY))
        operands.append(ctx_before)
        aliases = {6: 0}
    return pl.pallas_call(
        partial(forward_kernel, chunk),
        grid_spec=pltpu.PrefetchScalarGridSpec(
            num_scalar_prefetch=2,
            grid=(HEADS_PER_CHUNK,),
            in_specs=in_specs,
            out_specs=[
                pair_block(count, chunk * pairs),
                pl.BlockSpec((1, 1, count), lambda i, gate, ends: (i, 0, 0)),
            ],
            scratch_shapes=[pltpu.VMEM((count, count), f32), pltpu.VMEM((count, LANES), bf16)],
        ),
        out_shape=[
            jax.ShapeDtypeStruct((count, width), bf16),
            jax.ShapeDtypeStruct((HEADS_PER_CHUNK, 1, count), f32),
        ],
        input_output_aliases=aliases,
        compiler_params=pltpu.CompilerParams(vmem_limit_bytes=32 * 2**20),
        cost_estimate=pl.CostEstimate(
            flops=45 * count * count * HEAD * HEADS_PER_CHUNK,
            bytes_accessed=8 * count * LANES * pairs,
            transcendentals=count * count * HEADS_PER_CHUNK,
        ),
        name="attention_forward",
    )(*operands)


def backward_kernel(
    chunk, gate_ref, ends_ref, q_ref, k_ref, v_ref, do_ref, ctx_ref, lse_ref, valid_ref,
    grad_ref, sums_ref,
    bias_ref, qm_ref, dom_ref, dq_total, dk_total, dv_total, delta_ref,
):
    count = q_ref.shape[0]
    pairs = HEADS_PER_CHUNK // 2
    end_one, end_two = ends_ref[0], ends_ref[1]
    head = pl.program_id(0)
    keep = lanes_of(head)

    @pl.when(head == 0)
    def _():
        build_bias(bias_ref, valid_ref, end_one, end_two)

    @pl.when(head % 2 == 0)
    def _():
        dq_total[...] = jnp.zeros_like(dq_total)
        dk_total[...] = jnp.zeros_like(dk_total)
        dv_total[...] = jnp.zeros_like(dv_total)

    def step(index, carry):
        first_row = pl.multiple_of(index * QUERY_ROWS, QUERY_ROWS)
        queries = pl.ds(first_row, QUERY_ROWS)

        def body(width, start):
            window = pl.ds(start, width)
            keys, query, grad = k_ref[window, :], qm_ref[queries, :], dom_ref[queries, :]
            scores = dot_cols(keys, query) + bias_ref[window, queries]
            probs = jnp.exp(scores - lse_ref[0, :, queries])
            d_probs = dot_cols(v_ref[window, :], grad)
            d_scores = (probs * (d_probs - delta_ref[:, queries])).astype(bf16)
            dv_total[window, :] += dot(probs.astype(bf16), grad)
            dk_total[window, :] += dot(d_scores, query)
            d_query = (dot_rows(keys, d_scores) * HEAD**-0.5).T
            dq_total[queries, :] = jnp.where(keep, d_query, dq_total[queries, :])

        over_window(first_row, end_one, end_two, count, body)
        return carry

    @pl.when(gate_ref[chunk * HEADS_PER_CHUNK + head] > 0)
    def _():
        qm_ref[...] = jnp.where(keep, q_ref[...] * bf16(HEAD**-0.5), bf16(0))
        dom_ref[...] = jnp.where(keep, do_ref[...], bf16(0))
        product = dom_ref[...].astype(f32) * ctx_ref[...].astype(f32)
        delta_ref[...] = jnp.sum(product.T, axis=0, keepdims=True)
        lax.fori_loop(0, count // QUERY_ROWS, step, 0)

    @pl.when(head % 2 == 1)
    def _():
        for part, total in enumerate((dq_total, dk_total, dv_total)):
            low = total[...].astype(bf16)
            lanes = pl.ds(pl.multiple_of((part * pairs + head // 2) * LANES, LANES), LANES)
            grad_ref[:, lanes] = low
            if part != 1:
                sums_ref[part // 2 : part // 2 + 1, :] = jnp.sum(low.astype(f32), axis=0, keepdims=True)


def attention_backward(chunk, qkv, d_ctx, ctx, lse, valid_column, ends, gate):
    count, pairs = qkv.shape[0], HEADS_PER_CHUNK // 2
    return pl.pallas_call(
        partial(backward_kernel, chunk),
        grid_spec=pltpu.PrefetchScalarGridSpec(
            num_scalar_prefetch=2,
            grid=(HEADS_PER_CHUNK,),
            in_specs=[
                pair_block(count, 0),
                pair_block(count, pairs),
                pair_block(count, 2 * pairs),
                pair_block(count, chunk * pairs),
                pair_block(count, chunk * pairs),
                pl.BlockSpec((1, 1, count), lambda i, gate, ends: (i, 0, 0)),
                pl.BlockSpec((count, 1), lambda i, gate, ends: (0, 0)),
            ],
            out_specs=[
                pl.BlockSpec(qkv.shape, lambda i, gate, ends: (0, 0)),
                pl.BlockSpec((8, LANES), lambda i, gate, ends: (0, i // 2)),
            ],
            scratch_shapes=[
                pltpu.VMEM((count, count), f32),
                pltpu.VMEM((count, LANES), bf16),
                pltpu.VMEM((count, LANES), bf16),
                pltpu.VMEM((count, LANES), f32),
                pltpu.VMEM((count, LANES), f32),
                pltpu.VMEM((count, LANES), f32),
                pltpu.VMEM((1, count), f32),
            ],
        ),
        out_shape=[
            jax.ShapeDtypeStruct(qkv.shape, bf16),
            jax.ShapeDtypeStruct((8, pairs * LANES), f32),
        ],
        compiler_params=pltpu.CompilerParams(vmem_limit_bytes=40 * 2**20),
        cost_estimate=pl.CostEstimate(
            flops=45 * count * count * HEAD * HEADS_PER_CHUNK,
            bytes_accessed=16 * count * LANES * pairs,
            transcendentals=count * count * HEADS_PER_CHUNK,
        ),
        name="attention_backward",
    )(gate, ends, qkv, qkv, qkv, d_ctx, ctx, lse, valid_column)


def bits(size):
    return [1 << k for k in reversed(range(size.bit_length() - 1))]


def add_low(left, right):
    return (left.astype(f32) + right.astype(f32)).astype(bf16)


def hold(*values):
    return lax.optimization_barrier(values)


class Fabric:
    def __init__(self):
        self.dp, self.unit = lax.axis_size("dp"), lax.axis_size("unit")
        self.size = self.dp * self.unit
        self.at_unit = lax.axis_index("unit")
        self.at_dp = lax.axis_index("dp")
        self.me = self.at_dp * self.unit + self.at_unit
        dp_bits, unit_bits = [bit * self.unit for bit in bits(self.dp)], bits(self.unit)
        self.top, self.near, self.far, self.core = dp_bits[:-1], dp_bits[-1], unit_bits[:-1], unit_bits[-1]
        self.offsets = [0]
        for bit in self.far:
            self.offsets = self.offsets + [u ^ bit for u in self.offsets]

    def swap(self, value, bit):
        return lax.ppermute(value, AXES, [(i, i ^ bit) for i in range(self.size)])

    def assemble(self, parts, places):
        flat = jnp.stack([place for rows in places for place in rows]).astype(jnp.int32)

        def kernel(place_ref, *refs):
            index = 0
            for source in refs[:-1]:
                for row in range(source.shape[0]):
                    refs[-1][place_ref[index]] = source[row]
                    index += 1

        count, shape = flat.shape[0], parts[0].shape[1:]
        whole = pl.BlockSpec(memory_space=pltpu.VMEM)
        out = pl.pallas_call(
            kernel,
            in_specs=[pl.BlockSpec(memory_space=pltpu.SMEM)] + [whole] * len(parts),
            out_specs=whole,
            out_shape=jax.ShapeDtypeStruct((count, *shape), parts[0].dtype),
            compiler_params=pltpu.CompilerParams(vmem_limit_bytes=16 * 2**20),
            name="assemble",
        )(flat, *parts)
        return out.reshape(count * shape[0], shape[1])

    def split(self, value, bit, left):
        if bit in left:
            lower = 1 << sorted(left).index(bit)
            value = value.reshape(value.shape[0] // (2 * lower), 2, lower, *value.shape[1:])
            mine = (self.me // bit) % 2
            out = []
            for choice in (1 - mine, mine):
                half = lax.dynamic_index_in_dim(value, choice, 1, keepdims=False)
                out.append(half.reshape(-1, *half.shape[2:]))
            return tuple(out)
        half = value.shape[-1] // 2
        return value[..., half:], value[..., :half]

    def total(self, value):
        for bit in bits(self.size):
            value = value + self.swap(value, bit)
        return value

    def total_soon(self, value):
        steps = bits(self.size)[::-1]
        while steps:
            now, steps = steps[:3], steps[3:]
            masks = [0]
            for bit in now:
                masks = masks + [mask ^ bit for mask in masks]
            terms = [value if mask == 0 else self.swap(value, mask) for mask in masks]
            while len(terms) > 1:
                terms = [a + b for a, b in zip(terms[::2], terms[1::2])]
            value = terms[0]
        return value


class Gather:
    def __init__(self, fabric, block, masks):
        self.fabric, self.state, self.masks = fabric, block, masks

    def rows(self, bit):
        self.state = jnp.concatenate([self.state, self.fabric.swap(self.state, bit)])
        self.masks = self.masks + [mask ^ bit for mask in self.masks]

    def columns(self, bit):
        self.state = jnp.concatenate([self.state, self.fabric.swap(self.state, bit)], axis=-1)

    def place(self, shift, base):
        places = [base ^ (mask // shift) for mask in self.masks]
        self.state = self.fabric.assemble([self.state], [places])


class Scatter:
    def __init__(self, fabric, send, keep, bit, steps, rows):
        self.fabric, self.state, self.bit, self.steps = fabric, (send, keep), bit, list(steps)
        self.rows = [r for r in rows if r != bit]

    @classmethod
    def of(cls, fabric, grad, steps, rows):
        send, keep = fabric.split(grad, steps[0], rows)
        return cls(fabric, send, keep, steps[0], steps[1:], rows)

    def tick(self):
        send, keep = self.state
        other = self.fabric.swap(send, self.bit)
        if not self.steps:
            self.state = keep.astype(f32) + other.astype(f32)
            return
        self.bit = self.steps.pop(0)
        mine, theirs = (self.fabric.split(v, self.bit, self.rows) for v in (keep, other))
        self.rows = [r for r in self.rows if r != self.bit]
        self.state = tuple(add_low(a, b) for a, b in zip(mine, theirs))

    @classmethod
    def merge(cls, chains):
        first = chains[0]
        send, keep = (jnp.concatenate([c.state[i] for c in chains], axis=-1) for i in range(2))
        return cls(first.fabric, send, keep, first.bit, first.steps, first.rows)


def hold_all(values, chains):
    values, states = hold(values, [c.state for c in chains])
    for chain, state in zip(chains, states):
        chain.state = state
    return values


def normalize(value):
    mean = jnp.mean(value, axis=-1, keepdims=True)
    centred = value - mean
    root = lax.rsqrt(jnp.mean(centred * centred, axis=-1, keepdims=True) + EPS_NORM)
    return centred * root, root


def normalize_back(grad, hat, root, gain):
    scaled = grad * gain
    mean_one = jnp.mean(scaled, axis=-1, keepdims=True)
    mean_two = jnp.mean(scaled * hat, axis=-1, keepdims=True)
    back = root * (scaled - mean_one - hat * mean_two)
    return back, jnp.sum(grad * hat, axis=0), jnp.sum(grad, axis=0)


def adamw(master, first, second, grad, rate, decay):
    first_new = BETA_ONE * first + (1.0 - BETA_ONE) * grad
    second_new = BETA_TWO * second + (1.0 - BETA_TWO) * grad * grad
    first_hat = first_new / (1.0 - BETA_ONE**STEP)
    second_hat = second_new / (1.0 - BETA_TWO**STEP)
    master_new = master - rate * (first_hat / (jnp.sqrt(second_hat) + ADAM_EPS) + decay * master)
    return master_new, first_new, second_new


def shards(
    layer_input, teacher, cotangent, key_valid, seg_lengths, head_mask, hidden_mask, inter_mask,
    proj_master, proj_first, proj_second, up_master, up_first, up_second,
    down_master, down_first, down_second, vector_master, vector_first, vector_second,
):
    fabric = Fabric()
    top, near, far, core = fabric.top, fabric.near, fabric.far, fabric.core
    all_bits = top + [near] + far + [core]
    dp_bits = top + [near]
    rows, width = layer_input.shape
    chunks = head_mask.shape[0] // HEADS_PER_CHUNK
    span = HEADS_PER_CHUNK * HEAD
    hidden_gate = hidden_mask.astype(f32)
    valid = key_valid.astype(f32)[:, None]
    valid_column = key_valid[:, None]
    ends = jnp.cumsum(seg_lengths[0])
    head_gate = jnp.repeat(head_mask.astype(bf16), HEAD)
    vec = vector_master
    units = up_master.shape[1]

    def by_offset(values, offsets):
        return [
            lax.dynamic_index_in_dim(values, fabric.at_unit ^ u, 0, keepdims=False) for u in offsets
        ]

    def halves(values):
        values = values.reshape(fabric.unit, units)
        return [
            jnp.concatenate(by_offset(values, [u ^ flip for u in fabric.offsets]))
            for flip in (0, core)
        ]

    inner_bias = halves(vec[9:])
    unit_gate = halves(inter_mask.astype(f32))

    def by_chunk(matrix):
        return [
            matrix[..., p * width + c * span : p * width + (c + 1) * span]
            for c in range(chunks)
            for p in range(3)
        ]

    def gathered(block):
        return Gather(fabric, block, [0])

    proj_low = proj_master.astype(bf16)
    heads = gathered(jnp.concatenate(by_chunk(proj_low), axis=1)[None])
    ffn = gathered(jnp.concatenate([up_master.astype(bf16), down_master.astype(bf16).T])[None])
    outer = gathered(proj_low[None, :, 3 * width :])
    for bit in top:
        heads.rows(bit)
    for bit in top:
        ffn.rows(bit)
        outer.rows(bit)
    head_one = Gather(fabric, heads.state[:, :, : 3 * span], heads.masks)
    head_two = Gather(fabric, heads.state[:, :, 3 * span :], heads.masks)
    split = up_master.shape[0]
    up = Gather(fabric, ffn.state[:, :split], ffn.masks)
    down = Gather(fabric, ffn.state[:, split:], ffn.masks)
    head_one.rows(near)
    for bit in far:
        head_two.rows(bit)
        head_one.rows(bit)
    head_one.rows(core)
    head_two.rows(near)
    head_two.rows(core)
    head_one.place(1, fabric.me)
    head_two.place(1, fabric.me)
    up.rows(near)
    up.place(fabric.unit, fabric.at_dp)
    for bit in far:
        down.columns(bit)
    outer.rows(near)
    w_qkv = [head_one.state] + [
        head_two.state[:, c * 3 * span : (c + 1) * 3 * span] for c in range(chunks - 1)
    ]

    bias_qkv = jnp.concatenate(
        by_chunk(jnp.concatenate([vec[0], jnp.zeros_like(vec[0]), vec[1]]))
    ).reshape(chunks, 3 * span)

    def project(c):
        return (dot(layer_input, w_qkv[c]) + bias_qkv[c]).astype(bf16)

    def attend(c, ctx):
        return attention_forward(c, qkv[c], valid_column, ends, head_mask, ctx, width)

    qkv, lse, ctx = [project(0)], [], None
    (qkv[0],) = hold_all((qkv[0],), [up, down, outer])
    for bit in far:
        up.columns(bit)
        outer.rows(bit)
    down.rows(near)
    down.place(fabric.unit, fabric.at_dp)
    for c in range(chunks - 1):
        if c:
            qkv.append(project(c))
        ctx, part = attend(c, ctx)
        lse.append(part)
    qkv.append(project(chunks - 1))
    ctx, qkv[-1] = hold_all((ctx, qkv[-1]), [up, down, outer])
    w_up, w_down = [[g.state, fabric.swap(g.state, core)] for g in (up, down)]
    outer.rows(core)
    ctx, part = attend(chunks - 1, ctx)
    lse.append(part)
    outer.place(1, fabric.me)
    w_out, w_dist = outer.state[:, :width], outer.state[:, width:]

    attn = (dot(ctx, w_out) + vec[2]) * hidden_gate
    hat_one, root_one = normalize(layer_input.astype(f32) + attn)
    first = hat_one * vec[3] + vec[4]
    first_low = first.astype(bf16)
    branch, active, slope = vec[5], [], []
    for u in range(2):
        inner = dot(first_low, w_up[u]) + inner_bias[u]
        cdf = 0.5 * (1.0 + lax.erf(inner * 0.7071067811865476))
        pdf = jnp.exp(-0.5 * inner * inner) * 0.3989422804014327
        active.append((inner * cdf * unit_gate[u]).astype(bf16))
        slope.append(((cdf + inner * pdf) * unit_gate[u]).astype(bf16))
        branch = branch + dot_cols(active[u], w_down[u])
    hat_two, root_two = normalize(first + branch * hidden_gate)
    out_low = (hat_two * vec[6] + vec[7]).astype(bf16)
    error = dot(out_low, w_dist) + vec[8] - teacher.astype(f32)
    half_sq = 0.5 * jnp.sum(valid * error * error)
    d_student = (valid * error).astype(bf16)
    g_dist = dot_rows(out_low, d_student).astype(bf16)
    g_bias_dist = jnp.sum(d_student.astype(f32), axis=0)

    d_out = cotangent.astype(f32) + dot_cols(d_student, w_dist)
    d_second, g_gain_two, g_shift_two = normalize_back(d_out, hat_two, root_two, vec[6])
    d_branch = (d_second * hidden_gate).astype(bf16)
    g_bias_two = jnp.sum(d_branch.astype(f32), axis=0)
    d_first = d_second
    g_up, g_down, g_inner_bias = [None] * 2, [None] * 2, [None] * 2

    def tiles(grad):
        return grad.astype(bf16).reshape(fabric.dp, -1, grad.shape[1])

    for u in (1, 0):
        g_down[u] = tiles(dot_rows(d_branch, active[u]))
        d_inner = (dot(d_branch, w_down[u]) * slope[u].astype(f32)).astype(bf16)
        g_up[u] = tiles(dot_rows(first_low, d_inner))
        g_inner_bias[u] = jnp.sum(d_inner.astype(f32), axis=0)
        d_first = d_first + dot_cols(d_inner, w_up[u])
        if u:
            d_branch, d_first, g_up[1], g_down[1] = hold(d_branch, d_first, g_up[1], g_down[1])
    r_up = Scatter(fabric, g_up[1], g_up[0], core, far[::-1] + [near] + top[::-1], dp_bits)
    r_down = Scatter(fabric, g_down[1], g_down[0], core, [near] + far[::-1] + top[::-1], dp_bits)
    r_up.tick()
    r_down.tick()
    (d_first,) = hold_all((d_first,), [r_up, r_down])

    d_first_sum, g_gain_one, g_shift_one = normalize_back(d_first, hat_one, root_one, vec[3])
    d_attn = (d_first_sum * hidden_gate).astype(bf16)
    g_bias_out = jnp.sum(d_attn.astype(f32), axis=0)
    g_out = dot_rows(ctx, d_attn).astype(bf16)
    d_ctx = dot_cols(d_attn, w_out).astype(bf16) * head_gate
    input_grad, bias_sums = d_first_sum, []

    first_order = [core] + far[::-1] + [near] + top[::-1]
    second_order = [core, near] + far[::-1] + top[::-1]

    def scatter(grad, order):
        return Scatter.of(fabric, grad.reshape(fabric.size, -1, grad.shape[1]), order, all_bits)

    r_outer = scatter(jnp.concatenate([g_out, g_dist], axis=1), second_order)
    early = [r_up, r_down]
    r_qkv = []
    for c in range(chunks):
        for chain in early + r_qkv:
            if len(chain.steps) >= len(top):
                chain.tick()
        if c == 0:
            early.append(r_outer)
        d_qkv, sums = attention_backward(c, qkv[c], d_ctx, ctx, lse[c], valid_column, ends, head_mask)
        bias_sums.append(sums[:2])
        d_qkv, d_ctx = hold_all((d_qkv, d_ctx), early + r_qkv)
        grad = dot_rows(layer_input, d_qkv).astype(bf16)
        r_qkv.append(scatter(grad, second_order if c % 2 else first_order))
        input_grad = input_grad + dot_cols(d_qkv, w_qkv[c])
    r_ffn = Scatter.merge([r_up, r_down])
    last = r_qkv + [r_outer]
    while any(len(chain.steps) >= len(top) for chain in last):
        for chain in last:
            if len(chain.steps) >= len(top):
                chain.tick()
    r_proj = Scatter.merge(last)
    for _ in range(len(top)):
        r_ffn.tick()
        r_proj.tick()
    g_proj, g_ffn = r_proj.state[0], r_ffn.state[0]
    g_proj = jnp.concatenate(
        [
            g_proj[:, (c * 3 + p) * span : (c * 3 + p + 1) * span]
            for p in range(3)
            for c in range(chunks)
        ]
        + [g_proj[:, 3 * width :]],
        axis=1,
    )
    g_up, g_down = g_ffn[:, :units], g_ffn[:, units:]

    pieces = {}
    for flip, value in zip((0, core), g_inner_bias):
        for u, piece in zip(fabric.offsets, value.reshape(-1, units)):
            pieces[u ^ flip] = piece
    g_inner_bias = by_offset(jnp.stack([pieces[u] for u in range(fabric.unit)]), range(fabric.unit))
    vector_grad = jnp.concatenate(
        [
            jnp.concatenate(bias_sums, axis=1),
            jnp.stack(
                [g_bias_out, g_gain_one, g_shift_one, g_bias_two, g_gain_two, g_shift_two, g_bias_dist]
            ),
            jnp.stack(g_inner_bias).reshape(-1, width),
            jnp.full((1, width), half_sq),
        ]
    )
    vector_grad = fabric.total(vector_grad)
    half_total, vector_grad = vector_grad[-1, 0], vector_grad[:-1]
    shard_sq = jnp.sum(g_proj * g_proj) + jnp.sum(g_ffn * g_ffn)
    shard_total = fabric.total_soon(jnp.full((8, LANES), shard_sq))[0, 0]
    grad_norm = jnp.sqrt(shard_total + jnp.sum(vector_grad * vector_grad))
    clip = jnp.minimum(1.0, CLIP_NORM / (grad_norm + 1e-06))
    distill_loss = 2.0 * half_total / (rows * fabric.size * width)
    return (
        out_low,
        input_grad,
        grad_norm,
        distill_loss,
        *adamw(proj_master, proj_first, proj_second, clip * g_proj, RATE_MATRIX, DECAY_MATRIX),
        *adamw(up_master, up_first, up_second, clip * g_up, RATE_MATRIX, DECAY_MATRIX),
        *adamw(down_master, down_first, down_second, clip * g_down.T, RATE_MATRIX, DECAY_MATRIX),
        *adamw(vector_master, vector_first, vector_second, clip * vector_grad, RATE_VECTOR, 0.0),
    )


def solution(mesh):
    by_token = P(AXES, None)
    tile, tile_back = P("dp", "unit"), P("unit", "dp")
    in_specs = (
        (by_token, by_token, by_token, P(AXES), by_token, P(), P(), P())
        + (by_token,) * 3
        + (tile,) * 3
        + (tile_back,) * 3
        + (P(),) * 3
    )
    out_specs = (
        (by_token, by_token, P(), P()) + (by_token,) * 3 + (tile,) * 3 + (tile_back,) * 3 + (P(),) * 3
    )
    return jax.shard_map(shards, mesh=mesh, in_specs=in_specs, out_specs=out_specs, check_vma=False)
```

```python
from functools import partial

import jax
import jax.numpy as jnp
from jax import lax
from jax.experimental import pallas as pl
from jax.experimental.pallas import tpu as pltpu
from jax.sharding import PartitionSpec as P

STEP = 10
EPS_NORM = 1e-05
BETA_ONE = 0.9
BETA_TWO = 0.999
ADAM_EPS = 1e-08
RATE_MATRIX = 0.1
RATE_VECTOR = 1.0
DECAY_MATRIX = 0.01
CLIP_NORM = 1.0
HEAD = 64
LANES = 128
PAIRS_PER_CHUNK = 2
VMEM_BYTES = 24 * 2**20
BRIEF = pl.CostEstimate(flops=1000, bytes_accessed=1000, transcendentals=0)
QUERY_ROWS = 512
WIDTHS = (528, 656, 784, 912)
MASKED = -1e30
AXES = ("dp", "unit")
f32 = jnp.float32
bf16 = jnp.bfloat16


def dot(left, right):
    return jnp.dot(left, right, preferred_element_type=f32)


def dot_rows(left, right):
    return lax.dot_general(left, right, (((0,), (0,)), ((), ())), preferred_element_type=f32)


def dot_cols(left, right):
    return lax.dot_general(left, right, (((1,), (1,)), ((), ())), preferred_element_type=f32)


def build_bias(bias_ref, valid_ref, end_one, end_two):
    count = bias_ref.shape[0]
    for start in range(0, count, QUERY_ROWS):
        key = lax.broadcasted_iota(jnp.int32, (count, QUERY_ROWS), 0)
        query = lax.broadcasted_iota(jnp.int32, (count, QUERY_ROWS), 1) + start
        seg_key = (key >= end_one).astype(jnp.int32) + (key >= end_two).astype(jnp.int32)
        seg_query = (query >= end_one).astype(jnp.int32) + (query >= end_two).astype(jnp.int32)
        allowed = (seg_key == seg_query) & ((valid_ref[...] > 0) | (key == query))
        bias_ref[:, start : start + QUERY_ROWS] = jnp.where(allowed, 0.0, MASKED)


def over_window(first_row, end_one, end_two, count, body):
    low = jnp.where(first_row < end_one, 0, jnp.where(first_row < end_two, end_one, end_two))
    last_row = first_row + QUERY_ROWS - 1
    high = jnp.where(last_row < end_one, end_one, jnp.where(last_row < end_two, end_two, count))
    low = (low // 16) * 16
    done = jnp.bool_(False)
    for width in [w for w in WIDTHS if w < count] + [count]:
        start = jnp.minimum(low, count - width)
        fits = (high - start) <= width
        run = fits & jnp.logical_not(done)

        @pl.when(run)
        def _(width=width, start=start):
            body(width, pl.multiple_of(start, 16))

        done = done | fits


def lanes_of(member):
    return lax.broadcasted_iota(jnp.int32, (1, LANES), 1) // HEAD == member


def only(value, member):
    return jnp.where(lanes_of(member), value, bf16(0))


def by_member(upper, lower):
    row = lax.broadcasted_iota(jnp.int32, (LANES, 1), 0)
    return jnp.where(row < HEAD, upper, lower).T


def forward_kernel(chunk, gate_ref, ends_ref, q_ref, k_ref, v_ref, valid_ref, *refs):
    ctx_ref, lse_ref, bias_ref = refs[-3:]
    count = q_ref.shape[0]
    end_one, end_two = ends_ref[0], ends_ref[1]
    pair = pl.program_id(0)

    @pl.when(pair == 0)
    def _():
        build_bias(bias_ref, valid_ref, end_one, end_two)

    place = 2 * (chunk * PAIRS_PER_CHUNK + pair)
    gates = [gate_ref[place + member].astype(f32) for member in range(2)]
    gate = jnp.where(lanes_of(0), gates[0], gates[1])

    def step(index, carry):
        first_row = pl.multiple_of(index * QUERY_ROWS, QUERY_ROWS)
        queries = pl.ds(first_row, QUERY_ROWS)

        def body(width, start):
            window = pl.ds(start, width)
            query = q_ref[queries, :] * bf16(HEAD**-0.5)
            keys, bias, value = k_ref[window, :], bias_ref[window, queries], v_ref[window, :]
            outs = []
            for member in range(2):
                scores = dot_cols(keys, only(query, member)) + bias
                peak = jnp.max(scores, axis=0, keepdims=True)
                expo = jnp.exp(scores - peak)
                total = jnp.sum(expo, axis=0, keepdims=True)
                outs.append(dot_rows(value, expo.astype(bf16)) * (1.0 / total))
                lse_ref[member, :, queries] = peak + jnp.log(total)
            ctx_ref[queries, :] = (by_member(*outs) * gate).astype(bf16)

        over_window(first_row, end_one, end_two, count, body)
        return carry

    lax.fori_loop(0, count // QUERY_ROWS, step, 0)


def pair_block(count, offset):
    return pl.BlockSpec((count, LANES), lambda i, gate, ends: (0, i + offset))


def attention_forward(chunk, qkv, valid_column, ends, gate, ctx_before, width):
    count, pairs = qkv.shape[0], PAIRS_PER_CHUNK
    in_specs = [
        pair_block(count, 0),
        pair_block(count, pairs),
        pair_block(count, 2 * pairs),
        pl.BlockSpec((count, 1), lambda i, gate, ends: (0, 0)),
    ]
    operands = [gate, ends, qkv, qkv, qkv, valid_column]
    aliases = {}
    if ctx_before is not None:
        in_specs.append(pl.BlockSpec(memory_space=pl.ANY))
        operands.append(ctx_before)
        aliases = {6: 0}
    return pl.pallas_call(
        partial(forward_kernel, chunk),
        grid_spec=pltpu.PrefetchScalarGridSpec(
            num_scalar_prefetch=2,
            grid=(pairs,),
            in_specs=in_specs,
            out_specs=[
                pair_block(count, chunk * pairs),
                pl.BlockSpec((2, 1, count), lambda i, gate, ends: (i, 0, 0)),
            ],
            scratch_shapes=[pltpu.VMEM((count, count), f32)],
        ),
        out_shape=[
            jax.ShapeDtypeStruct((count, width), bf16),
            jax.ShapeDtypeStruct((2 * pairs, 1, count), f32),
        ],
        input_output_aliases=aliases,
        compiler_params=pltpu.CompilerParams(vmem_limit_bytes=VMEM_BYTES),
        cost_estimate=BRIEF,
        name="attention_forward",
    )(*operands)


def backward_kernel(
    chunk, ends_ref, q_ref, k_ref, v_ref, do_ref, ctx_ref, lse_ref, valid_ref,
    grad_ref, sums_ref,
    bias_ref, dq_low, dk_total, dv_total, delta_ref,
):
    count = q_ref.shape[0]
    end_one, end_two = ends_ref[0], ends_ref[1]
    pair = pl.program_id(0)

    @pl.when(pair == 0)
    def _():
        build_bias(bias_ref, valid_ref, end_one, end_two)

    dk_total[...] = jnp.zeros_like(dk_total)
    dv_total[...] = jnp.zeros_like(dv_total)
    product = (do_ref[...].astype(f32) * ctx_ref[...].astype(f32)).T
    for member in range(2):
        rows = product[member * HEAD : (member + 1) * HEAD]
        delta_ref[member : member + 1, :] = jnp.sum(rows, axis=0, keepdims=True)

    def step(index, carry):
        first_row = pl.multiple_of(index * QUERY_ROWS, QUERY_ROWS)
        queries = pl.ds(first_row, QUERY_ROWS)

        def body(width, start):
            window = pl.ds(start, width)
            keys, value, bias = k_ref[window, :], v_ref[window, :], bias_ref[window, queries]
            query, grad = q_ref[queries, :] * bf16(HEAD**-0.5), do_ref[queries, :]
            d_queries, all_probs, all_scores, all_query, all_grad = [], [], [], [], []
            for member in range(2):
                own_query, own_grad = only(query, member), only(grad, member)
                probs = jnp.exp(dot_cols(keys, own_query) + bias - lse_ref[member, :, queries])
                d_probs = dot_cols(value, own_grad)
                d_scores = (probs * (d_probs - delta_ref[member : member + 1, queries])).astype(bf16)
                all_probs.append(probs.astype(bf16))
                all_scores.append(d_scores)
                all_query.append(own_query)
                all_grad.append(own_grad)
                d_queries.append(dot_rows(keys, d_scores))
            dv_total[window, :] += dot(
                jnp.concatenate(all_probs, axis=1), jnp.concatenate(all_grad, axis=0)
            )
            dk_total[window, :] += dot(
                jnp.concatenate(all_scores, axis=1), jnp.concatenate(all_query, axis=0)
            )
            dq_low[queries, :] = (by_member(*d_queries) * HEAD**-0.5).astype(bf16)

        over_window(first_row, end_one, end_two, count, body)
        return carry

    lax.fori_loop(0, count // QUERY_ROWS, step, 0)
    parts = (dq_low[...], dk_total[...].astype(bf16), dv_total[...].astype(bf16))
    for part, low in enumerate(parts):
        at = (part * PAIRS_PER_CHUNK + pair) * LANES
        grad_ref[:, pl.ds(pl.multiple_of(at, LANES), LANES)] = low
        if part != 1:
            sums_ref[part // 2 : part // 2 + 1, :] = jnp.sum(low.astype(f32), axis=0, keepdims=True)


def attention_backward(chunk, qkv, d_ctx, ctx, lse, valid_column, ends):
    count, pairs = qkv.shape[0], PAIRS_PER_CHUNK

    def block(offset):
        return pl.BlockSpec((count, LANES), lambda i, ends: (0, i + offset))

    return pl.pallas_call(
        partial(backward_kernel, chunk),
        grid_spec=pltpu.PrefetchScalarGridSpec(
            num_scalar_prefetch=1,
            grid=(pairs,),
            in_specs=[
                block(0),
                block(pairs),
                block(2 * pairs),
                block(chunk * pairs),
                block(chunk * pairs),
                pl.BlockSpec((2, 1, count), lambda i, ends: (i, 0, 0)),
                pl.BlockSpec((count, 1), lambda i, ends: (0, 0)),
            ],
            out_specs=[
                pl.BlockSpec(qkv.shape, lambda i, ends: (0, 0)),
                pl.BlockSpec((8, LANES), lambda i, ends: (0, i)),
            ],
            scratch_shapes=[
                pltpu.VMEM((count, count), f32),
                pltpu.VMEM((count, LANES), bf16),
                pltpu.VMEM((count, LANES), f32),
                pltpu.VMEM((count, LANES), f32),
                pltpu.VMEM((8, count), f32),
            ],
        ),
        out_shape=[
            jax.ShapeDtypeStruct(qkv.shape, bf16),
            jax.ShapeDtypeStruct((8, pairs * LANES), f32),
        ],
        compiler_params=pltpu.CompilerParams(vmem_limit_bytes=VMEM_BYTES),
        cost_estimate=BRIEF,
        name="attention_backward",
    )(ends, qkv, qkv, qkv, d_ctx, ctx, lse, valid_column)


def bits(size):
    return [1 << k for k in reversed(range(size.bit_length() - 1))]


def add_low(left, right):
    return (left.astype(f32) + right.astype(f32)).astype(bf16)


def hold(*values):
    return lax.optimization_barrier(values)


def hold(*values):
    return lax.optimization_barrier(values)


class Fabric:
    def __init__(self):
        self.dp, self.unit = lax.axis_size("dp"), lax.axis_size("unit")
        self.size = self.dp * self.unit
        self.at_unit = lax.axis_index("unit")
        self.at_dp = lax.axis_index("dp")
        self.me = self.at_dp * self.unit + self.at_unit
        dp_bits, unit_bits = [bit * self.unit for bit in bits(self.dp)], bits(self.unit)
        self.top, self.near, self.far, self.core = dp_bits[:-1], dp_bits[-1], unit_bits[:-1], unit_bits[-1]
        self.offsets = [0]
        for bit in self.far:
            self.offsets = self.offsets + [u ^ bit for u in self.offsets]

    def swap(self, value, bit):
        return lax.ppermute(value, AXES, [(i, i ^ bit) for i in range(self.size)])

    def assemble(self, block, places):
        flat = jnp.stack(places).astype(jnp.int32)

        def kernel(place_ref, source, out):
            for row in range(source.shape[0]):
                out[place_ref[row]] = source[row]

        whole = pl.BlockSpec(memory_space=pltpu.VMEM)
        out = pl.pallas_call(
            kernel,
            in_specs=[pl.BlockSpec(memory_space=pltpu.SMEM), whole],
            out_specs=whole,
            out_shape=jax.ShapeDtypeStruct(block.shape, block.dtype),
            compiler_params=pltpu.CompilerParams(vmem_limit_bytes=16 * 2**20),
            name="assemble",
        )(flat, block)
        return out.reshape(-1, block.shape[2])

    def by_device(self, block, masks):
        return self.assemble(block, [self.me ^ mask for mask in masks])

    def split(self, value, bit, left):
        own = bit if bit in left else -bit
        lower = 1 << (len(left) - 1 - left.index(own))
        value = value.reshape(value.shape[0] // (2 * lower), 2, lower, *value.shape[1:])
        mine = (self.me // bit) % 2 if own > 0 else 0
        out = []
        for choice in (1 - mine, mine):
            half = lax.dynamic_index_in_dim(value, choice, 1, keepdims=False)
            out.append(half.reshape(-1, *half.shape[2:]))
        return tuple(out)

    def total(self, value):
        for bit in bits(self.size)[::-1]:
            value = value + self.swap(value, bit)
        return value


def doubled(fabric, block, masks, bit):
    return jnp.concatenate([block, fabric.swap(block, bit)]), masks + [mask ^ bit for mask in masks]


class Scatter:
    def __init__(self, fabric, send, keep, steps, left):
        self.fabric, self.send, self.keep, self.steps = fabric, send, keep, list(steps)
        self.left = [r for r in left if abs(r) != steps[0]]

    @classmethod
    def of(cls, fabric, grad, steps, left):
        return cls(fabric, *fabric.split(grad, steps[0], left), steps, left)

    def start(self):
        self.other = self.fabric.swap(self.send, self.steps.pop(0))

    def finish(self):
        if not self.steps:
            self.result = (self.keep.astype(f32) + self.other.astype(f32))[0]
            return
        bit = self.steps[0]
        mine, theirs = (self.fabric.split(v, bit, self.left) for v in (self.keep, self.other))
        self.left = [r for r in self.left if abs(r) != bit]
        self.send, self.keep = (
            (a.astype(f32) + b.astype(f32)).astype(bf16) for a, b in zip(mine, theirs)
        )

    @classmethod
    def merge(cls, chains):
        first = chains[0]
        send, keep = (
            jnp.concatenate([getattr(c, name) for c in chains], axis=-1) for name in ("send", "keep")
        )
        return cls(first.fabric, send, keep, first.steps, first.left + first.steps[:1])


def beside(chains, compute):
    for chain in chains:
        chain.start()
    values, others = hold(compute(), [chain.other for chain in chains])
    for chain, other in zip(chains, others):
        chain.other = other
        chain.finish()
    return values


ROWS = 256


def row_call(kernel, count, blocks, constants, outs, sums, scratch, name):
    steps = count // ROWS

    def by_row(a):
        return pl.BlockSpec((ROWS, a.shape[1]), lambda i: (i, 0))

    def whole(a):
        return pl.BlockSpec(a.shape, lambda i: (0,) * len(a.shape))

    return pl.pallas_call(
        partial(kernel, steps),
        grid=(steps,),
        in_specs=[by_row(a) for a in blocks] + [whole(a) for a in constants],
        out_specs=[by_row(a) for a in outs] + [whole(a) for a in sums],
        out_shape=list(outs) + list(sums),
        scratch_shapes=scratch,
        compiler_params=pltpu.CompilerParams(vmem_limit_bytes=VMEM_BYTES),
        cost_estimate=BRIEF,
        name=name,
    )(*blocks, *constants)


def column_sums(value):
    return jnp.sum(value, axis=0, keepdims=True)


def normalize(value):
    mean = jnp.mean(value, axis=-1, keepdims=True)
    centred = value - mean
    root = lax.rsqrt(jnp.mean(centred * centred, axis=-1, keepdims=True) + EPS_NORM)
    return centred * root, root


def normalize_back(grad, hat, root, gain):
    scaled = grad * gain
    mean_one = jnp.mean(scaled, axis=-1, keepdims=True)
    mean_two = jnp.mean(scaled * hat, axis=-1, keepdims=True)
    return root * (scaled - mean_one - hat * mean_two)


def attention_out_kernel(steps, ctx, x, w_out, vec, gate, hat_out, root_out, low_out):
    attn = (dot(ctx[...], w_out[...]) + vec[2:3, :]) * gate[...]
    hat, root = normalize(x[...].astype(f32) + attn)
    hat_out[...] = hat
    root_out[...] = root
    low_out[...] = (hat * vec[3:4, :] + vec[4:5, :]).astype(bf16)


def head_kernel(
    steps, branch, hat_one, teacher, cotangent, valid, w_dist, vec, gate,
    low_out, d_second_out, d_branch_out, sums, g_dist, total,
):
    step = pl.program_id(0)

    @pl.when(step == 0)
    def _():
        sums[...] = jnp.zeros_like(sums)
        total[...] = jnp.zeros_like(total)

    keep = (valid[...] > 0).astype(f32)
    first = hat_one[...] * vec[3:4, :] + vec[4:5, :]
    hat, root = normalize(first + (branch[...] + vec[5:6, :]) * gate[...])
    low = (hat * vec[6:7, :] + vec[7:8, :]).astype(bf16)
    low_out[...] = low
    error = dot(low, w_dist[...]) + vec[8:9, :] - teacher[...].astype(f32)
    kept = keep * error
    d_student = kept.astype(bf16)
    d_out = cotangent[...].astype(f32) + dot_cols(d_student, w_dist[...])
    d_second = normalize_back(d_out, hat, root, vec[6:7, :])
    d_second_out[...] = d_second
    d_branch = (d_second * gate[...]).astype(bf16)
    d_branch_out[...] = d_branch
    sums[0:1, :] += column_sums(d_student.astype(f32))
    sums[1:2, :] += column_sums(d_out * hat)
    sums[2:3, :] += column_sums(d_out)
    sums[3:4, :] += column_sums(d_branch.astype(f32))
    sums[4:5, :] += column_sums(kept * error)
    total[...] += dot_rows(low, d_student)

    @pl.when(step == steps - 1)
    def _():
        g_dist[...] = total[...].astype(bf16)


def attention_out_back_kernel(
    steps, d_first, hat_one, root_one, ctx, w_out, vec, gate, head_gate,
    d_sum_out, d_ctx_out, sums, g_out, total,
):
    step = pl.program_id(0)

    @pl.when(step == 0)
    def _():
        sums[...] = jnp.zeros_like(sums)
        total[...] = jnp.zeros_like(total)

    hat, grad = hat_one[...], d_first[...]
    d_sum = normalize_back(grad, hat, root_one[...], vec[3:4, :])
    d_sum_out[...] = d_sum
    d_attn = (d_sum * gate[...]).astype(bf16)
    d_ctx_out[...] = (dot_cols(d_attn, w_out[...]) * head_gate[...]).astype(bf16)
    sums[0:1, :] += column_sums(d_attn.astype(f32))
    sums[1:2, :] += column_sums(grad * hat)
    sums[2:3, :] += column_sums(grad)
    total[...] += dot_rows(ctx[...], d_attn)

    @pl.when(step == steps - 1)
    def _():
        g_out[...] = total[...].astype(bf16)


def input_grad_kernel(steps, before, d_qkv, weight, out):
    out[...] = before[...] + dot_cols(d_qkv[...], weight[...])


def adamw(master, first, second, grad, rate, decay):
    first_new = BETA_ONE * first + (1.0 - BETA_ONE) * grad
    second_new = BETA_TWO * second + (1.0 - BETA_TWO) * grad * grad
    first_hat = first_new / (1.0 - BETA_ONE**STEP)
    second_hat = second_new / (1.0 - BETA_TWO**STEP)
    master_new = master - rate * (first_hat / (jnp.sqrt(second_hat) + ADAM_EPS) + decay * master)
    return master_new, first_new, second_new


def shards(
    layer_input, teacher, cotangent, key_valid, seg_lengths, head_mask, hidden_mask, inter_mask,
    proj_master, proj_first, proj_second, up_master, up_first, up_second,
    down_master, down_first, down_second, vector_master, vector_first, vector_second,
):
    fabric = Fabric()
    top, near, far, core = fabric.top, fabric.near, fabric.far, fabric.core
    all_bits = top + [near] + far + [core]
    rows, width = layer_input.shape
    span = PAIRS_PER_CHUNK * LANES
    chunks = width // span
    hidden_gate = hidden_mask.astype(f32)[None]
    valid_column = key_valid[:, None]
    ends = jnp.cumsum(seg_lengths[0])
    head_gate = jnp.repeat(head_mask.astype(f32), HEAD)[None]
    vec = vector_master
    tile_rows, units = up_master.shape

    offsets = fabric.offsets + [u ^ core for u in fabric.offsets]

    def by_offset(values, order):
        return [lax.dynamic_index_in_dim(values, fabric.at_unit ^ u, 0, keepdims=False) for u in order]

    inner_bias = by_offset(vec[9:].reshape(fabric.unit, units), offsets)
    unit_gate = by_offset(inter_mask.astype(f32).reshape(fabric.unit, units), offsets)

    def by_chunk(matrix):
        return [
            matrix[..., p * width + c * span : p * width + (c + 1) * span]
            for c in range(chunks)
            for p in range(3)
        ]

    proj_low = proj_master.astype(bf16)
    block, masks = jnp.concatenate(by_chunk(proj_low), axis=1)[None], [0]
    for bit in top:
        block, masks = doubled(fabric, block, masks, bit)
    ones, ones_masks, twos, twos_masks = block[..., : 3 * span], masks, block[..., 3 * span :], masks
    for bit in [near] + far + [core]:
        ones, ones_masks = doubled(fabric, ones, ones_masks, bit)
    for bit in far + [near]:
        twos, twos_masks = doubled(fabric, twos, twos_masks, bit)
    w_qkv = [fabric.by_device(ones, ones_masks)]

    rest = jnp.concatenate(
        [
            up_master.astype(bf16),
            down_master.astype(bf16).T,
            proj_low[:, 3 * width : 4 * width].reshape(-1, units),
            proj_low[:, 4 * width :].reshape(-1, units),
        ]
    )
    rest = lax.all_gather(rest, ("unit", "dp"), axis=0).reshape(fabric.unit, fabric.dp, -1, units)
    count = (rest.shape[2] - 2 * tile_rows) // 2


    def tile(u, at):
        size = (1, fabric.dp, tile_rows, units)
        return lax.dynamic_slice(rest, (fabric.at_unit ^ u, 0, at, 0), size).reshape(width, units)

    w_up, w_down = ([tile(u, at) for u in offsets] for at in (0, tile_rows))
    w_out, w_dist = (
        rest[:, :, at : at + count].transpose(1, 0, 2, 3).reshape(width, width)
        for at in (2 * tile_rows, 2 * tile_rows + count)
    )

    bias_qkv = jnp.concatenate(
        by_chunk(jnp.concatenate([vec[0], jnp.zeros_like(vec[0]), vec[1]]))
    ).reshape(chunks, 3 * span)

    def project(c):
        return (dot(layer_input, w_qkv[c]) + bias_qkv[c]).astype(bf16)

    qkv, lse, ctx = [project(0)], [], None

    def attend(ctx):
        c = len(lse)
        ctx, part = attention_forward(c, qkv[c], valid_column, ends, head_mask, ctx, width)
        lse.append(part)
        return ctx

    qkv[0], twos = hold(qkv[0], twos)
    other = fabric.swap(twos, core)
    ctx, other = hold(attend(ctx), other)
    late = fabric.by_device(
        jnp.concatenate([twos, other]), twos_masks + [mask ^ core for mask in twos_masks]
    )
    w_qkv += [late[:, c * 3 * span : (c + 1) * 3 * span] for c in range(chunks - 1)]
    for c in range(1, chunks):
        qkv.append(project(c))
        ctx = attend(ctx)

    def like(kind, *shape):
        return jax.ShapeDtypeStruct(shape or (rows, width), kind)

    hat_one, root_one, first_low = row_call(
        attention_out_kernel, rows, [ctx, layer_input], [w_out, vec, hidden_gate],
        [like(f32), like(f32, rows, 1), like(bf16)], [], [], "attention_out",
    )
    branch, active, slope = 0.0, [], []
    for u in range(fabric.unit):
        inner = dot(first_low, w_up[u]) + inner_bias[u]
        cdf = 0.5 * (1.0 + lax.erf(inner * 0.7071067811865476))
        pdf = jnp.exp(-0.5 * inner * inner) * 0.3989422804014327
        active.append((inner * cdf * unit_gate[u]).astype(bf16))
        slope.append((cdf + inner * pdf) * unit_gate[u])
        branch = branch + dot_cols(active[u], w_down[u])
    out_low, d_second, d_branch, head_sums, g_dist = row_call(
        head_kernel, rows, [branch, hat_one, teacher, cotangent, valid_column],
        [w_dist, vec, hidden_gate], [like(bf16), like(f32), like(bf16)],
        [like(f32, 8, width), like(bf16, width, width)],
        [pltpu.VMEM((width, width), f32)], "head",
    )

    unit_bits, dp_bits = far + [core], top + [near]
    blocks = len(fabric.offsets)
    block_bits = [-bit for bit in far[::-1]] + dp_bits

    def stacked(grads):
        return jnp.stack(grads).reshape(blocks * fabric.dp, tile_rows, units)

    def g_blocks(make):
        return [stacked([make(u) for u in side]) for side in (range(blocks, 2 * blocks), range(blocks))]

    g_down = g_blocks(lambda u: dot_rows(d_branch, active[u]).astype(bf16))
    r_down = Scatter(fabric, *g_down, [core, near] + far[::-1] + top[::-1], [core] + block_bits)
    r_down.start()
    d_inner = [(dot(d_branch, w_down[u]) * slope[u]).astype(bf16) for u in range(2 * blocks)]
    g_up = g_blocks(lambda u: dot_rows(first_low, d_inner[u]).astype(bf16))
    g_inner_bias = [jnp.sum(d.astype(f32), axis=0) for d in d_inner]
    *g_up, r_down.other = hold(*g_up, r_down.other)
    r_down.finish()
    r_up = Scatter(fabric, *g_up, [core] + far[::-1] + [near] + top[::-1], [core] + block_bits)
    order = [core] + far[::-1] + [near] + top[::-1]

    def feed_forward_back():
        return sum((dot_cols(d_inner[u], w_up[u]) for u in range(2 * blocks)), d_second)

    def attention_out_back():
        return row_call(
            attention_out_back_kernel, rows, [d_first, hat_one, root_one, ctx],
            [w_out, vec, hidden_gate, head_gate], [like(f32), like(bf16)],
            [like(f32, 8, width), like(bf16, width, width)],
            [pltpu.VMEM((width, width), f32)], "attention_out_back",
        )

    def attend_back(c):
        return attention_backward(c, qkv[c], d_ctx, ctx, lse[c], valid_column, ends)

    def add_input_grad(c):
        if c >= chunks:
            return [input_grad]
        return row_call(
            input_grad_kernel, rows, [input_grad, d_qkv[c]], [w_qkv[c]], [like(f32)], [], [], "input_grad"
        )

    def scatter(grad):
        grad = grad.reshape(fabric.size, -1, grad.shape[1])
        return Scatter.of(fabric, grad, order, dp_bits + unit_bits)

    r_down.start()
    d_first = beside([r_up], feed_forward_back)
    d_qkv, bias_sums, chains = [], [], []
    for c in range(chunks):
        if c == 0:

            def compute():
                global_parts = attention_out_back()
                return global_parts, attention_backward(
                    0, qkv[0], global_parts[1], ctx, lse[0], valid_column, ends
                )

            r_up.start()
            (d_first_sum, d_ctx, out_sums, g_out), (grad, sums) = compute()
            grad, d_ctx, r_up.other, r_down.other = hold(grad, d_ctx, r_up.other, r_down.other)
            r_up.finish()
            r_down.finish()
            rings = [r_up, r_down]
        else:
            while len(rings[0].steps) > len(top) + 1:
                beside(rings, lambda: 0)
            grad, sums = beside(rings + chains, lambda: attend_back(c))
            if len(rings) > 1 and len(rings[0].steps) == len(top):
                rings = [Scatter.merge(rings)]
        d_qkv.append(grad)
        bias_sums.append(sums[:2])
        mine = dot_rows(layer_input, grad).astype(bf16)
        if c == 0:
            mine = jnp.concatenate([mine, g_out, g_dist], axis=1)
        chains.append(scatter(mine))
    input_grad, c = d_first_sum, 0
    while len(chains[-1].steps) > len(top):
        busy = [chain for chain in rings + chains if chain.steps]
        (input_grad,) = beside(busy, lambda: add_input_grad(c))
        c += 1
    while c < chunks:
        (input_grad,) = add_input_grad(c)
        c += 1
    late = [chain for chain in chains if len(chain.steps) == len(top)]
    done = [chain for chain in chains if len(chain.steps) < len(top)]
    last = Scatter.merge(late)
    while last.steps:
        beside([chain for chain in rings + [last] + done if chain.steps], lambda: 0)
    results, at = [chain.result for chain in done], 0
    for chain in late:
        size = chain.keep.shape[-1]
        results.append(last.result[:, at : at + size])
        at += size
    g_proj = jnp.concatenate(
        [result[:, p * span : (p + 1) * span] for p in range(3) for result in results]
        + [results[0][:, 3 * span :]],
        axis=1,
    )
    g_up, g_down = rings[0].result[:, :units], rings[0].result[:, units:]
    g_inner_bias = dict(zip(offsets, g_inner_bias))
    g_inner_bias = by_offset(jnp.stack([g_inner_bias[u] for u in range(fabric.unit)]), range(fabric.unit))

    squares = sum(jnp.sum(g * g) for g in (g_proj, g_up, g_down))
    table = jnp.concatenate(
        [
            jnp.concatenate(bias_sums, axis=1),
            out_sums[:3],
            head_sums[3:4],
            head_sums[1:3],
            head_sums[:1],
            jnp.stack(g_inner_bias).reshape(-1, width),
            head_sums[4:5],
            jnp.full((1, width), squares),
        ]
    )
    table = fabric.total(table)
    vector_grad, error_total, square_total = table[:-2], jnp.sum(table[-2]), table[-1, 0]
    grad_norm = jnp.sqrt(square_total + jnp.sum(vector_grad * vector_grad))
    clip = jnp.minimum(1.0, CLIP_NORM / (grad_norm + 1e-06))
    distill_loss = error_total / (rows * fabric.size * width)
    return (
        out_low,
        input_grad,
        grad_norm,
        distill_loss,
        *adamw(proj_master, proj_first, proj_second, clip * g_proj, RATE_MATRIX, DECAY_MATRIX),
        *adamw(up_master, up_first, up_second, clip * g_up, RATE_MATRIX, DECAY_MATRIX),
        *adamw(down_master, down_first, down_second, clip * g_down.T, RATE_MATRIX, DECAY_MATRIX),
        *adamw(vector_master, vector_first, vector_second, clip * vector_grad, RATE_VECTOR, 0.0),
    )


def solution(mesh):
    by_token = P(AXES, None)
    tile, tile_back = P("dp", "unit"), P("unit", "dp")
    in_specs = (
        (by_token, by_token, by_token, P(AXES), by_token, P(), P(), P())
        + (by_token,) * 3
        + (tile,) * 3
        + (tile_back,) * 3
        + (P(),) * 3
    )
    out_specs = (
        (by_token, by_token, P(), P()) + (by_token,) * 3 + (tile,) * 3 + (tile_back,) * 3 + (P(),) * 3
    )
    return jax.shard_map(shards, mesh=mesh, in_specs=in_specs, out_specs=out_specs, check_vma=False)
```

```python
from functools import partial

import jax
import jax.numpy as jnp
from jax import lax
from jax.experimental import pallas as pl
from jax.experimental.pallas import tpu as pltpu
from jax.sharding import PartitionSpec as P

STEP = 10
EPS_NORM = 1e-05
BETA_ONE = 0.9
BETA_TWO = 0.999
ADAM_EPS = 1e-08
RATE_MATRIX = 0.1
RATE_VECTOR = 1.0
DECAY_MATRIX = 0.01
CLIP_NORM = 1.0
HEAD = 64
LANES = 128
PAIRS_PER_CHUNK = 2
VMEM_BYTES = 24 * 2**20
BRIEF = pl.CostEstimate(flops=1000, bytes_accessed=1000, transcendentals=0)
QUERY_ROWS = 512
WIDTHS = (528, 656, 784, 912)
MASKED = -1e30
AXES = ("dp", "unit")
f32 = jnp.float32
bf16 = jnp.bfloat16


def dot(left, right):
    return jnp.dot(left, right, preferred_element_type=f32)


def dot_rows(left, right):
    return lax.dot_general(left, right, (((0,), (0,)), ((), ())), preferred_element_type=f32)


def dot_cols(left, right):
    return lax.dot_general(left, right, (((1,), (1,)), ((), ())), preferred_element_type=f32)


def build_bias(bias_ref, valid_ref, end_one, end_two):
    count = bias_ref.shape[0]
    for start in range(0, count, QUERY_ROWS):
        key = lax.broadcasted_iota(jnp.int32, (count, QUERY_ROWS), 0)
        query = lax.broadcasted_iota(jnp.int32, (count, QUERY_ROWS), 1) + start
        seg_key = (key >= end_one).astype(jnp.int32) + (key >= end_two).astype(jnp.int32)
        seg_query = (query >= end_one).astype(jnp.int32) + (query >= end_two).astype(jnp.int32)
        allowed = (seg_key == seg_query) & ((valid_ref[...] > 0) | (key == query))
        bias_ref[:, start : start + QUERY_ROWS] = jnp.where(allowed, 0.0, MASKED)


def over_window(first_row, end_one, end_two, count, body):
    low = jnp.where(first_row < end_one, 0, jnp.where(first_row < end_two, end_one, end_two))
    last_row = first_row + QUERY_ROWS - 1
    high = jnp.where(last_row < end_one, end_one, jnp.where(last_row < end_two, end_two, count))
    low = (low // 16) * 16
    done = jnp.bool_(False)
    for width in [w for w in WIDTHS if w < count] + [count]:
        start = jnp.minimum(low, count - width)
        fits = (high - start) <= width
        run = fits & jnp.logical_not(done)

        @pl.when(run)
        def _(width=width, start=start):
            body(width, pl.multiple_of(start, 16))

        done = done | fits


def lanes_of(member):
    return lax.broadcasted_iota(jnp.int32, (1, LANES), 1) // HEAD == member


def only(value, member):
    return jnp.where(lanes_of(member), value, bf16(0))


def by_member(upper, lower):
    row = lax.broadcasted_iota(jnp.int32, (LANES, 1), 0)
    return jnp.where(row < HEAD, upper, lower).T


def forward_kernel(chunk, gate_ref, ends_ref, q_ref, k_ref, v_ref, valid_ref, *refs):
    ctx_ref, lse_ref, bias_ref = refs[-3:]
    count = q_ref.shape[0]
    end_one, end_two = ends_ref[0], ends_ref[1]
    pair = pl.program_id(0)

    @pl.when(pair == 0)
    def _():
        build_bias(bias_ref, valid_ref, end_one, end_two)

    place = 2 * (chunk * PAIRS_PER_CHUNK + pair)
    gates = [gate_ref[place + member].astype(f32) for member in range(2)]
    gate = jnp.where(lanes_of(0), gates[0], gates[1])

    def step(index, carry):
        first_row = pl.multiple_of(index * QUERY_ROWS, QUERY_ROWS)
        queries = pl.ds(first_row, QUERY_ROWS)

        def body(width, start):
            window = pl.ds(start, width)
            query = q_ref[queries, :] * bf16(HEAD**-0.5)
            keys, bias, value = k_ref[window, :], bias_ref[window, queries], v_ref[window, :]
            outs = []
            for member in range(2):
                scores = dot_cols(keys, only(query, member)) + bias
                peak = jnp.max(scores, axis=0, keepdims=True)
                expo = jnp.exp(scores - peak)
                total = jnp.sum(expo, axis=0, keepdims=True)
                outs.append(dot_rows(value, expo.astype(bf16)) * (1.0 / total))
                lse_ref[member, :, queries] = peak + jnp.log(total)
            ctx_ref[queries, :] = (by_member(*outs) * gate).astype(bf16)

        over_window(first_row, end_one, end_two, count, body)
        return carry

    lax.fori_loop(0, count // QUERY_ROWS, step, 0)


def pair_block(count, offset):
    return pl.BlockSpec((count, LANES), lambda i, gate, ends: (0, i + offset))


def attention_forward(chunk, qkv, valid_column, ends, gate, ctx_before, width):
    count, pairs = qkv.shape[0], PAIRS_PER_CHUNK
    in_specs = [
        pair_block(count, 0),
        pair_block(count, pairs),
        pair_block(count, 2 * pairs),
        pl.BlockSpec((count, 1), lambda i, gate, ends: (0, 0)),
    ]
    operands = [gate, ends, qkv, qkv, qkv, valid_column]
    aliases = {}
    if ctx_before is not None:
        in_specs.append(pl.BlockSpec(memory_space=pl.ANY))
        operands.append(ctx_before)
        aliases = {6: 0}
    return pl.pallas_call(
        partial(forward_kernel, chunk),
        grid_spec=pltpu.PrefetchScalarGridSpec(
            num_scalar_prefetch=2,
            grid=(pairs,),
            in_specs=in_specs,
            out_specs=[
                pair_block(count, chunk * pairs),
                pl.BlockSpec((2, 1, count), lambda i, gate, ends: (i, 0, 0)),
            ],
            scratch_shapes=[pltpu.VMEM((count, count), f32)],
        ),
        out_shape=[
            jax.ShapeDtypeStruct((count, width), bf16),
            jax.ShapeDtypeStruct((2 * pairs, 1, count), f32),
        ],
        input_output_aliases=aliases,
        compiler_params=pltpu.CompilerParams(vmem_limit_bytes=VMEM_BYTES),
        cost_estimate=BRIEF,
        name="attention_forward",
    )(*operands)


def backward_kernel(
    chunk, ends_ref, q_ref, k_ref, v_ref, do_ref, ctx_ref, lse_ref, valid_ref,
    grad_ref, sums_ref,
    bias_ref, dq_low, dk_total, dv_total, delta_ref,
):
    count = q_ref.shape[0]
    end_one, end_two = ends_ref[0], ends_ref[1]
    pair = pl.program_id(0)

    @pl.when(pair == 0)
    def _():
        build_bias(bias_ref, valid_ref, end_one, end_two)

    dk_total[...] = jnp.zeros_like(dk_total)
    dv_total[...] = jnp.zeros_like(dv_total)
    product = (do_ref[...].astype(f32) * ctx_ref[...].astype(f32)).T
    for member in range(2):
        rows = product[member * HEAD : (member + 1) * HEAD]
        delta_ref[member : member + 1, :] = jnp.sum(rows, axis=0, keepdims=True)

    def step(index, carry):
        first_row = pl.multiple_of(index * QUERY_ROWS, QUERY_ROWS)
        queries = pl.ds(first_row, QUERY_ROWS)

        def body(width, start):
            window = pl.ds(start, width)
            keys, value, bias = k_ref[window, :], v_ref[window, :], bias_ref[window, queries]
            query, grad = q_ref[queries, :] * bf16(HEAD**-0.5), do_ref[queries, :]
            d_queries, all_probs, all_scores, all_query, all_grad = [], [], [], [], []
            for member in range(2):
                own_query, own_grad = only(query, member), only(grad, member)
                probs = jnp.exp(dot_cols(keys, own_query) + bias - lse_ref[member, :, queries])
                d_probs = dot_cols(value, own_grad)
                d_scores = (probs * (d_probs - delta_ref[member : member + 1, queries])).astype(bf16)
                all_probs.append(probs.astype(bf16))
                all_scores.append(d_scores)
                all_query.append(own_query)
                all_grad.append(own_grad)
                d_queries.append(dot_rows(keys, d_scores))
            dv_total[window, :] += dot(
                jnp.concatenate(all_probs, axis=1), jnp.concatenate(all_grad, axis=0)
            )
            dk_total[window, :] += dot(
                jnp.concatenate(all_scores, axis=1), jnp.concatenate(all_query, axis=0)
            )
            dq_low[queries, :] = (by_member(*d_queries) * HEAD**-0.5).astype(bf16)

        over_window(first_row, end_one, end_two, count, body)
        return carry

    lax.fori_loop(0, count // QUERY_ROWS, step, 0)
    parts = (dq_low[...], dk_total[...].astype(bf16), dv_total[...].astype(bf16))
    for part, low in enumerate(parts):
        at = (part * PAIRS_PER_CHUNK + pair) * LANES
        grad_ref[:, pl.ds(pl.multiple_of(at, LANES), LANES)] = low
        if part != 1:
            sums_ref[part // 2 : part // 2 + 1, :] = jnp.sum(low.astype(f32), axis=0, keepdims=True)


def attention_backward(chunk, qkv, d_ctx, ctx, lse, valid_column, ends):
    count, pairs = qkv.shape[0], PAIRS_PER_CHUNK

    def block(offset):
        return pl.BlockSpec((count, LANES), lambda i, ends: (0, i + offset))

    return pl.pallas_call(
        partial(backward_kernel, chunk),
        grid_spec=pltpu.PrefetchScalarGridSpec(
            num_scalar_prefetch=1,
            grid=(pairs,),
            in_specs=[
                block(0),
                block(pairs),
                block(2 * pairs),
                block(chunk * pairs),
                block(chunk * pairs),
                pl.BlockSpec((2, 1, count), lambda i, ends: (i, 0, 0)),
                pl.BlockSpec((count, 1), lambda i, ends: (0, 0)),
            ],
            out_specs=[
                pl.BlockSpec(qkv.shape, lambda i, ends: (0, 0)),
                pl.BlockSpec((8, LANES), lambda i, ends: (0, i)),
            ],
            scratch_shapes=[
                pltpu.VMEM((count, count), f32),
                pltpu.VMEM((count, LANES), bf16),
                pltpu.VMEM((count, LANES), f32),
                pltpu.VMEM((count, LANES), f32),
                pltpu.VMEM((8, count), f32),
            ],
        ),
        out_shape=[
            jax.ShapeDtypeStruct(qkv.shape, bf16),
            jax.ShapeDtypeStruct((8, pairs * LANES), f32),
        ],
        compiler_params=pltpu.CompilerParams(vmem_limit_bytes=VMEM_BYTES),
        cost_estimate=BRIEF,
        name="attention_backward",
    )(ends, qkv, qkv, qkv, d_ctx, ctx, lse, valid_column)


def bits(size):
    return [1 << k for k in reversed(range(size.bit_length() - 1))]


def add_low(left, right):
    return (left.astype(f32) + right.astype(f32)).astype(bf16)


def hold(*values):
    return lax.optimization_barrier(values)


def hold(*values):
    return lax.optimization_barrier(values)


class Fabric:
    def __init__(self):
        self.dp, self.unit = lax.axis_size("dp"), lax.axis_size("unit")
        self.size = self.dp * self.unit
        self.at_unit = lax.axis_index("unit")
        self.at_dp = lax.axis_index("dp")
        self.me = self.at_dp * self.unit + self.at_unit
        dp_bits, unit_bits = [bit * self.unit for bit in bits(self.dp)], bits(self.unit)
        self.top, self.near, self.far, self.core = dp_bits[:-1], dp_bits[-1], unit_bits[:-1], unit_bits[-1]
        self.offsets = [0]
        for bit in self.far:
            self.offsets = self.offsets + [u ^ bit for u in self.offsets]

    def swap(self, value, bit):
        return lax.ppermute(value, AXES, [(i, i ^ bit) for i in range(self.size)])

    def assemble(self, block, places):
        flat = jnp.stack(places).astype(jnp.int32)

        def kernel(place_ref, source, out):
            for row in range(source.shape[0]):
                out[place_ref[row]] = source[row]

        whole = pl.BlockSpec(memory_space=pltpu.VMEM)
        out = pl.pallas_call(
            kernel,
            in_specs=[pl.BlockSpec(memory_space=pltpu.SMEM), whole],
            out_specs=whole,
            out_shape=jax.ShapeDtypeStruct(block.shape, block.dtype),
            compiler_params=pltpu.CompilerParams(vmem_limit_bytes=16 * 2**20),
            name="assemble",
        )(flat, block)
        return out.reshape(-1, block.shape[2])

    def by_device(self, block, masks):
        return self.assemble(block, [self.me ^ mask for mask in masks])

    def split(self, value, bit, left):
        own = bit if bit in left else -bit
        lower = 1 << (len(left) - 1 - left.index(own))
        value = value.reshape(value.shape[0] // (2 * lower), 2, lower, *value.shape[1:])
        mine = (self.me // bit) % 2 if own > 0 else 0
        out = []
        for choice in (1 - mine, mine):
            half = lax.dynamic_index_in_dim(value, choice, 1, keepdims=False)
            out.append(half.reshape(-1, *half.shape[2:]))
        return tuple(out)

    def total(self, value):
        for bit in bits(self.size)[::-1]:
            value = value + self.swap(value, bit)
        return value


def doubled(fabric, block, masks, bit):
    return jnp.concatenate([block, fabric.swap(block, bit)]), masks + [mask ^ bit for mask in masks]


class Scatter:
    def __init__(self, fabric, send, keep, steps, left):
        self.fabric, self.send, self.keep, self.steps = fabric, send, keep, list(steps)
        self.left = [r for r in left if abs(r) != steps[0]]

    @classmethod
    def of(cls, fabric, grad, steps, left):
        return cls(fabric, *fabric.split(grad, steps[0], left), steps, left)

    def start(self):
        self.other = self.fabric.swap(self.send, self.steps.pop(0))

    def finish(self):
        if not self.steps:
            self.result = (self.keep.astype(f32) + self.other.astype(f32))[0]
            return
        bit = self.steps[0]
        mine, theirs = (self.fabric.split(v, bit, self.left) for v in (self.keep, self.other))
        self.left = [r for r in self.left if abs(r) != bit]
        self.send, self.keep = (
            (a.astype(f32) + b.astype(f32)).astype(bf16) for a, b in zip(mine, theirs)
        )

    @classmethod
    def merge(cls, chains):
        first = chains[0]
        send, keep = (
            jnp.concatenate([getattr(c, name) for c in chains], axis=-1) for name in ("send", "keep")
        )
        return cls(first.fabric, send, keep, first.steps, first.left + first.steps[:1])


def beside(chains, compute):
    for chain in chains:
        chain.start()
    values, others = hold(compute(), [chain.other for chain in chains])
    for chain, other in zip(chains, others):
        chain.other = other
        chain.finish()
    return values


ROWS = 256


def row_call(kernel, count, blocks, constants, outs, sums, scratch, name):
    steps = count // ROWS

    def by_row(a):
        return pl.BlockSpec((ROWS, a.shape[1]), lambda i: (i, 0))

    def whole(a):
        return pl.BlockSpec(a.shape, lambda i: (0,) * len(a.shape))

    return pl.pallas_call(
        partial(kernel, steps),
        grid=(steps,),
        in_specs=[by_row(a) for a in blocks] + [whole(a) for a in constants],
        out_specs=[by_row(a) for a in outs] + [whole(a) for a in sums],
        out_shape=list(outs) + list(sums),
        scratch_shapes=scratch,
        compiler_params=pltpu.CompilerParams(vmem_limit_bytes=VMEM_BYTES),
        cost_estimate=BRIEF,
        name=name,
    )(*blocks, *constants)


def column_sums(value):
    return jnp.sum(value, axis=0, keepdims=True)


def normalize(value):
    mean = jnp.mean(value, axis=-1, keepdims=True)
    centred = value - mean
    root = lax.rsqrt(jnp.mean(centred * centred, axis=-1, keepdims=True) + EPS_NORM)
    return centred * root, root


def normalize_back(grad, hat, root, gain):
    scaled = grad * gain
    mean_one = jnp.mean(scaled, axis=-1, keepdims=True)
    mean_two = jnp.mean(scaled * hat, axis=-1, keepdims=True)
    return root * (scaled - mean_one - hat * mean_two)


def attention_out_kernel(steps, ctx, x, w_out, vec, gate, hat_out, root_out, low_out):
    attn = (dot(ctx[...], w_out[...]) + vec[2:3, :]) * gate[...]
    hat, root = normalize(x[...].astype(f32) + attn)
    hat_out[...] = hat
    root_out[...] = root
    low_out[...] = (hat * vec[3:4, :] + vec[4:5, :]).astype(bf16)


def head_kernel(
    steps, branch, hat_one, teacher, cotangent, valid, w_dist, vec, gate,
    low_out, d_second_out, d_branch_out, sums, g_dist, total,
):
    step = pl.program_id(0)

    @pl.when(step == 0)
    def _():
        sums[...] = jnp.zeros_like(sums)
        total[...] = jnp.zeros_like(total)

    keep = (valid[...] > 0).astype(f32)
    first = hat_one[...] * vec[3:4, :] + vec[4:5, :]
    hat, root = normalize(first + (branch[...] + vec[5:6, :]) * gate[...])
    low = (hat * vec[6:7, :] + vec[7:8, :]).astype(bf16)
    low_out[...] = low
    error = dot(low, w_dist[...]) + vec[8:9, :] - teacher[...].astype(f32)
    kept = keep * error
    d_student = kept.astype(bf16)
    d_out = cotangent[...].astype(f32) + dot_cols(d_student, w_dist[...])
    d_second = normalize_back(d_out, hat, root, vec[6:7, :])
    d_second_out[...] = d_second
    d_branch = (d_second * gate[...]).astype(bf16)
    d_branch_out[...] = d_branch
    sums[0:1, :] += column_sums(d_student.astype(f32))
    sums[1:2, :] += column_sums(d_out * hat)
    sums[2:3, :] += column_sums(d_out)
    sums[3:4, :] += column_sums(d_branch.astype(f32))
    sums[4:5, :] += column_sums(kept * error)
    total[...] += dot_rows(low, d_student)

    @pl.when(step == steps - 1)
    def _():
        g_dist[...] = total[...].astype(bf16)


def attention_out_back_kernel(
    steps, d_first, hat_one, root_one, ctx, w_out, vec, gate, head_gate,
    d_sum_out, d_ctx_out, sums, g_out, total,
):
    step = pl.program_id(0)

    @pl.when(step == 0)
    def _():
        sums[...] = jnp.zeros_like(sums)
        total[...] = jnp.zeros_like(total)

    hat, grad = hat_one[...], d_first[...]
    d_sum = normalize_back(grad, hat, root_one[...], vec[3:4, :])
    d_sum_out[...] = d_sum
    d_attn = (d_sum * gate[...]).astype(bf16)
    d_ctx_out[...] = (dot_cols(d_attn, w_out[...]) * head_gate[...]).astype(bf16)
    sums[0:1, :] += column_sums(d_attn.astype(f32))
    sums[1:2, :] += column_sums(grad * hat)
    sums[2:3, :] += column_sums(grad)
    total[...] += dot_rows(ctx[...], d_attn)

    @pl.when(step == steps - 1)
    def _():
        g_out[...] = total[...].astype(bf16)


def input_grad_kernel(steps, before, d_qkv, weight, out):
    out[...] = before[...] + dot_cols(d_qkv[...], weight[...])


def adamw(master, first, second, grad, rate, decay):
    first_new = BETA_ONE * first + (1.0 - BETA_ONE) * grad
    second_new = BETA_TWO * second + (1.0 - BETA_TWO) * grad * grad
    first_hat = first_new / (1.0 - BETA_ONE**STEP)
    second_hat = second_new / (1.0 - BETA_TWO**STEP)
    master_new = master - rate * (first_hat / (jnp.sqrt(second_hat) + ADAM_EPS) + decay * master)
    return master_new, first_new, second_new


def shards(
    layer_input, teacher, cotangent, key_valid, seg_lengths, head_mask, hidden_mask, inter_mask,
    proj_master, proj_first, proj_second, up_master, up_first, up_second,
    down_master, down_first, down_second, vector_master, vector_first, vector_second,
):
    fabric = Fabric()
    top, near, far, core = fabric.top, fabric.near, fabric.far, fabric.core
    all_bits = top + [near] + far + [core]
    rows, width = layer_input.shape
    span = PAIRS_PER_CHUNK * LANES
    chunks = width // span
    hidden_gate = hidden_mask.astype(f32)[None]
    valid_column = key_valid[:, None]
    ends = jnp.cumsum(seg_lengths[0])
    head_gate = jnp.repeat(head_mask.astype(f32), HEAD)[None]
    vec = vector_master
    tile_rows, units = up_master.shape

    offsets = fabric.offsets + [u ^ core for u in fabric.offsets]

    def by_offset(values, order):
        return [lax.dynamic_index_in_dim(values, fabric.at_unit ^ u, 0, keepdims=False) for u in order]

    inner_bias = by_offset(vec[9:].reshape(fabric.unit, units), offsets)
    unit_gate = by_offset(inter_mask.astype(f32).reshape(fabric.unit, units), offsets)

    def by_chunk(matrix):
        return [
            matrix[..., p * width + c * span : p * width + (c + 1) * span]
            for c in range(chunks)
            for p in range(3)
        ]

    proj_low = proj_master.astype(bf16)
    block, masks = jnp.concatenate(by_chunk(proj_low), axis=1)[None], [0]
    for bit in top:
        block, masks = doubled(fabric, block, masks, bit)
    ones, ones_masks, twos, twos_masks = block[..., : 3 * span], masks, block[..., 3 * span :], masks
    for bit in [near] + far + [core]:
        ones, ones_masks = doubled(fabric, ones, ones_masks, bit)
    for bit in far + [near]:
        twos, twos_masks = doubled(fabric, twos, twos_masks, bit)
    w_qkv = [fabric.by_device(ones, ones_masks)]

    rest = jnp.concatenate(
        [
            up_master.astype(bf16),
            down_master.astype(bf16).T,
            proj_low[:, 3 * width : 4 * width].reshape(-1, units),
            proj_low[:, 4 * width :].reshape(-1, units),
        ]
    )
    rest = lax.all_gather(rest, AXES, axis=0).reshape(fabric.dp, fabric.unit, -1, units)
    count = (rest.shape[2] - 2 * tile_rows) // 2

    def tile(u, at):
        size = (fabric.dp, 1, tile_rows, units)
        return lax.dynamic_slice(rest, (0, fabric.at_unit ^ u, at, 0), size).reshape(width, units)

    w_up, w_down = ([tile(u, at) for u in offsets] for at in (0, tile_rows))
    w_out, w_dist = (
        rest[:, :, at : at + count].reshape(width, width)
        for at in (2 * tile_rows, 2 * tile_rows + count)
    )

    bias_qkv = jnp.concatenate(
        by_chunk(jnp.concatenate([vec[0], jnp.zeros_like(vec[0]), vec[1]]))
    ).reshape(chunks, 3 * span)

    def project(c):
        return (dot(layer_input, w_qkv[c]) + bias_qkv[c]).astype(bf16)

    qkv, lse, ctx = [project(0)], [], None

    def attend(ctx):
        c = len(lse)
        ctx, part = attention_forward(c, qkv[c], valid_column, ends, head_mask, ctx, width)
        lse.append(part)
        return ctx

    qkv[0], twos = hold(qkv[0], twos)
    other = fabric.swap(twos, core)
    ctx, other = hold(attend(ctx), other)
    late = fabric.by_device(
        jnp.concatenate([twos, other]), twos_masks + [mask ^ core for mask in twos_masks]
    )
    w_qkv += [late[:, c * 3 * span : (c + 1) * 3 * span] for c in range(chunks - 1)]
    for c in range(1, chunks):
        qkv.append(project(c))
        ctx = attend(ctx)

    def like(kind, *shape):
        return jax.ShapeDtypeStruct(shape or (rows, width), kind)

    hat_one, root_one, first_low = row_call(
        attention_out_kernel, rows, [ctx, layer_input], [w_out, vec, hidden_gate],
        [like(f32), like(f32, rows, 1), like(bf16)], [], [], "attention_out",
    )
    branch, active, slope = 0.0, [], []
    for u in range(fabric.unit):
        inner = dot(first_low, w_up[u]) + inner_bias[u]
        cdf = 0.5 * (1.0 + lax.erf(inner * 0.7071067811865476))
        pdf = jnp.exp(-0.5 * inner * inner) * 0.3989422804014327
        active.append((inner * cdf * unit_gate[u]).astype(bf16))
        slope.append((cdf + inner * pdf) * unit_gate[u])
        branch = branch + dot_cols(active[u], w_down[u])
    out_low, d_second, d_branch, head_sums, g_dist = row_call(
        head_kernel, rows, [branch, hat_one, teacher, cotangent, valid_column],
        [w_dist, vec, hidden_gate], [like(bf16), like(f32), like(bf16)],
        [like(f32, 8, width), like(bf16, width, width)],
        [pltpu.VMEM((width, width), f32)], "head",
    )

    unit_bits, dp_bits = far + [core], top + [near]
    blocks = len(fabric.offsets)
    block_bits = [-bit for bit in far[::-1]] + dp_bits

    def stacked(grads):
        return jnp.stack(grads).reshape(blocks * fabric.dp, tile_rows, units)

    def g_blocks(make):
        return [stacked([make(u) for u in side]) for side in (range(blocks, 2 * blocks), range(blocks))]

    g_down = g_blocks(lambda u: dot_rows(d_branch, active[u]).astype(bf16))
    r_down = Scatter(fabric, *g_down, [core, near] + far[::-1] + top[::-1], [core] + block_bits)
    r_down.start()
    d_inner = [(dot(d_branch, w_down[u]) * slope[u]).astype(bf16) for u in range(2 * blocks)]
    g_up = g_blocks(lambda u: dot_rows(first_low, d_inner[u]).astype(bf16))
    g_inner_bias = [jnp.sum(d.astype(f32), axis=0) for d in d_inner]
    *g_up, r_down.other = hold(*g_up, r_down.other)
    r_down.finish()
    r_up = Scatter(fabric, *g_up, [core] + far[::-1] + [near] + top[::-1], [core] + block_bits)
    order = [core] + far[::-1] + [near] + top[::-1]

    def feed_forward_back():
        return sum((dot_cols(d_inner[u], w_up[u]) for u in range(2 * blocks)), d_second)

    def attention_out_back():
        return row_call(
            attention_out_back_kernel, rows, [d_first, hat_one, root_one, ctx],
            [w_out, vec, hidden_gate, head_gate], [like(f32), like(bf16)],
            [like(f32, 8, width), like(bf16, width, width)],
            [pltpu.VMEM((width, width), f32)], "attention_out_back",
        )

    def attend_back(c):
        return attention_backward(c, qkv[c], d_ctx, ctx, lse[c], valid_column, ends)

    def add_input_grad(c):
        if c >= chunks:
            return [input_grad]
        return row_call(
            input_grad_kernel, rows, [input_grad, d_qkv[c]], [w_qkv[c]], [like(f32)], [], [], "input_grad"
        )

    def scatter(grad):
        grad = grad.reshape(fabric.size, -1, grad.shape[1])
        return Scatter.of(fabric, grad, order, dp_bits + unit_bits)

    r_down.start()
    d_first = beside([r_up], feed_forward_back)
    d_qkv, bias_sums, chains = [], [], []
    for c in range(chunks):
        if c == 0:

            def compute():
                global_parts = attention_out_back()
                return global_parts, attention_backward(
                    0, qkv[0], global_parts[1], ctx, lse[0], valid_column, ends
                )

            r_up.start()
            (d_first_sum, d_ctx, out_sums, g_out), (grad, sums) = compute()
            grad, d_ctx, r_up.other, r_down.other = hold(grad, d_ctx, r_up.other, r_down.other)
            r_up.finish()
            r_down.finish()
            rings = [r_up, r_down]
        else:
            while len(rings[0].steps) > len(top) + 1:
                beside(rings, lambda: 0)
            grad, sums = beside(rings + chains, lambda: attend_back(c))
            if len(rings) > 1 and len(rings[0].steps) == len(top):
                rings = [Scatter.merge(rings)]
        d_qkv.append(grad)
        bias_sums.append(sums[:2])
        mine = dot_rows(layer_input, grad).astype(bf16)
        if c == 0:
            mine = jnp.concatenate([mine, g_out, g_dist], axis=1)
        chains.append(scatter(mine))
    input_grad, c = d_first_sum, 0
    while len(chains[-1].steps) > len(top):
        busy = [chain for chain in rings + chains if chain.steps]
        (input_grad,) = beside(busy, lambda: add_input_grad(c))
        c += 1
    while c < chunks:
        (input_grad,) = add_input_grad(c)
        c += 1
    late = [chain for chain in chains if len(chain.steps) == len(top)]
    done = [chain for chain in chains if len(chain.steps) < len(top)]
    last = Scatter.merge(late)
    while last.steps:
        beside([chain for chain in rings + [last] + done if chain.steps], lambda: 0)
    results, at = [chain.result for chain in done], 0
    for chain in late:
        size = chain.keep.shape[-1]
        results.append(last.result[:, at : at + size])
        at += size
    g_proj = jnp.concatenate(
        [result[:, p * span : (p + 1) * span] for p in range(3) for result in results]
        + [results[0][:, 3 * span :]],
        axis=1,
    )
    g_up, g_down = rings[0].result[:, :units], rings[0].result[:, units:]
    g_inner_bias = dict(zip(offsets, g_inner_bias))
    g_inner_bias = by_offset(jnp.stack([g_inner_bias[u] for u in range(fabric.unit)]), range(fabric.unit))

    squares = sum(jnp.sum(g * g) for g in (g_proj, g_up, g_down))
    table = jnp.concatenate(
        [
            jnp.concatenate(bias_sums, axis=1),
            out_sums[:3],
            head_sums[3:4],
            head_sums[1:3],
            head_sums[:1],
            jnp.stack(g_inner_bias).reshape(-1, width),
            head_sums[4:5],
            jnp.full((1, width), squares),
        ]
    )
    table = fabric.total(table)
    vector_grad, error_total, square_total = table[:-2], jnp.sum(table[-2]), table[-1, 0]
    grad_norm = jnp.sqrt(square_total + jnp.sum(vector_grad * vector_grad))
    clip = jnp.minimum(1.0, CLIP_NORM / (grad_norm + 1e-06))
    distill_loss = error_total / (rows * fabric.size * width)
    return (
        out_low,
        input_grad,
        grad_norm,
        distill_loss,
        *adamw(proj_master, proj_first, proj_second, clip * g_proj, RATE_MATRIX, DECAY_MATRIX),
        *adamw(up_master, up_first, up_second, clip * g_up, RATE_MATRIX, DECAY_MATRIX),
        *adamw(down_master, down_first, down_second, clip * g_down.T, RATE_MATRIX, DECAY_MATRIX),
        *adamw(vector_master, vector_first, vector_second, clip * vector_grad, RATE_VECTOR, 0.0),
    )


def solution(mesh):
    by_token = P(AXES, None)
    tile, tile_back = P("dp", "unit"), P("unit", "dp")
    in_specs = (
        (by_token, by_token, by_token, P(AXES), by_token, P(), P(), P())
        + (by_token,) * 3
        + (tile,) * 3
        + (tile_back,) * 3
        + (P(),) * 3
    )
    out_specs = (
        (by_token, by_token, P(), P()) + (by_token,) * 3 + (tile,) * 3 + (tile_back,) * 3 + (P(),) * 3
    )
    return jax.shard_map(shards, mesh=mesh, in_specs=in_specs, out_specs=out_specs, check_vma=False)
```

```python
from functools import partial

import jax
import jax.numpy as jnp
from jax import lax
from jax.experimental import pallas as pl
from jax.experimental.pallas import tpu as pltpu
from jax.sharding import PartitionSpec as P

STEP = 10
EPS_NORM = 1e-05
BETA_ONE = 0.9
BETA_TWO = 0.999
ADAM_EPS = 1e-08
RATE_MATRIX = 0.1
RATE_VECTOR = 1.0
DECAY_MATRIX = 0.01
CLIP_NORM = 1.0
HEAD = 64
LANES = 128
PAIRS_PER_CHUNK = 2
VMEM_BYTES = 24 * 2**20
BRIEF = pl.CostEstimate(flops=1000, bytes_accessed=1000, transcendentals=0)
QUERY_ROWS = 512
WIDTHS = (528, 784)
BACK_WIDTHS = (528, 656, 784, 912)
MASKED = -1e30
AXES = ("dp", "unit")
f32 = jnp.float32
bf16 = jnp.bfloat16


def dot(left, right):
    return jnp.dot(left, right, preferred_element_type=f32)


def dot_rows(left, right):
    return lax.dot_general(left, right, (((0,), (0,)), ((), ())), preferred_element_type=f32)


def dot_cols(left, right):
    return lax.dot_general(left, right, (((1,), (1,)), ((), ())), preferred_element_type=f32)


def build_bias(bias_ref, valid_ref, end_one, end_two):
    count = bias_ref.shape[0]
    for start in range(0, count, QUERY_ROWS):
        key = lax.broadcasted_iota(jnp.int32, (count, QUERY_ROWS), 0)
        query = lax.broadcasted_iota(jnp.int32, (count, QUERY_ROWS), 1) + start
        seg_key = (key >= end_one).astype(jnp.int32) + (key >= end_two).astype(jnp.int32)
        seg_query = (query >= end_one).astype(jnp.int32) + (query >= end_two).astype(jnp.int32)
        allowed = (seg_key == seg_query) & ((valid_ref[...] > 0) | (key == query))
        bias_ref[:, start : start + QUERY_ROWS] = jnp.where(allowed, 0.0, MASKED)


def over_window(first_row, end_one, end_two, count, body, widths=WIDTHS):
    low = jnp.where(first_row < end_one, 0, jnp.where(first_row < end_two, end_one, end_two))
    last_row = first_row + QUERY_ROWS - 1
    high = jnp.where(last_row < end_one, end_one, jnp.where(last_row < end_two, end_two, count))
    low = (low // 16) * 16
    done = jnp.bool_(False)
    for width in [w for w in widths if w < count] + [count]:
        start = jnp.minimum(low, count - width)
        fits = (high - start) <= width
        run = fits & jnp.logical_not(done)

        @pl.when(run)
        def _(width=width, start=start):
            body(width, pl.multiple_of(start, 16))

        done = done | fits


def lanes_of(member):
    return lax.broadcasted_iota(jnp.int32, (1, LANES), 1) // HEAD == member


def only(value, member):
    return jnp.where(lanes_of(member), value, bf16(0))


def by_member(upper, lower):
    row = lax.broadcasted_iota(jnp.int32, (LANES, 1), 0)
    return jnp.where(row < HEAD, upper, lower).T


def forward_kernel(chunk, gate_ref, ends_ref, q_ref, k_ref, v_ref, valid_ref, *refs):
    ctx_ref, lse_ref, bias_ref = refs[-3:]
    count = q_ref.shape[0]
    end_one, end_two = ends_ref[0], ends_ref[1]
    pair = pl.program_id(0)

    @pl.when(pair == 0)
    def _():
        build_bias(bias_ref, valid_ref, end_one, end_two)

    place = 2 * (chunk * PAIRS_PER_CHUNK + pair)
    gates = [gate_ref[place + member].astype(f32) for member in range(2)]
    gate = jnp.where(lanes_of(0), gates[0], gates[1])

    def step(index, carry):
        first_row = pl.multiple_of(index * QUERY_ROWS, QUERY_ROWS)
        queries = pl.ds(first_row, QUERY_ROWS)

        def body(width, start):
            window = pl.ds(start, width)
            query = q_ref[queries, :] * bf16(HEAD**-0.5)
            keys, bias, value = k_ref[window, :], bias_ref[window, queries], v_ref[window, :]
            outs = []
            for member in range(2):
                scores = dot_cols(keys, only(query, member)) + bias
                peak = jnp.max(scores, axis=0, keepdims=True)
                expo = jnp.exp(scores - peak)
                total = jnp.sum(expo, axis=0, keepdims=True)
                outs.append(dot_rows(value, expo.astype(bf16)) * (1.0 / total))
                lse_ref[member, :, queries] = peak + jnp.log(total)
            ctx_ref[queries, :] = (by_member(*outs) * gate).astype(bf16)

        over_window(first_row, end_one, end_two, count, body)
        return carry

    lax.fori_loop(0, count // QUERY_ROWS, step, 0)


def pair_block(count, offset):
    return pl.BlockSpec((count, LANES), lambda i, gate, ends: (0, i + offset))


def attention_forward(chunk, qkv, valid_column, ends, gate, ctx_before, width):
    count, pairs = qkv.shape[0], PAIRS_PER_CHUNK
    in_specs = [
        pair_block(count, 0),
        pair_block(count, pairs),
        pair_block(count, 2 * pairs),
        pl.BlockSpec((count, 1), lambda i, gate, ends: (0, 0)),
    ]
    operands = [gate, ends, qkv, qkv, qkv, valid_column]
    aliases = {}
    if ctx_before is not None:
        in_specs.append(pl.BlockSpec(memory_space=pl.ANY))
        operands.append(ctx_before)
        aliases = {6: 0}
    return pl.pallas_call(
        partial(forward_kernel, chunk),
        grid_spec=pltpu.PrefetchScalarGridSpec(
            num_scalar_prefetch=2,
            grid=(pairs,),
            in_specs=in_specs,
            out_specs=[
                pair_block(count, chunk * pairs),
                pl.BlockSpec((2, 1, count), lambda i, gate, ends: (i, 0, 0)),
            ],
            scratch_shapes=[pltpu.VMEM((count, count), f32)],
        ),
        out_shape=[
            jax.ShapeDtypeStruct((count, width), bf16),
            jax.ShapeDtypeStruct((2 * pairs, 1, count), f32),
        ],
        input_output_aliases=aliases,
        compiler_params=pltpu.CompilerParams(vmem_limit_bytes=VMEM_BYTES),
        cost_estimate=BRIEF,
        name="attention_forward",
    )(*operands)


def backward_kernel(
    chunk, ends_ref, q_ref, k_ref, v_ref, do_ref, ctx_ref, lse_ref, valid_ref,
    grad_ref, sums_ref,
    bias_ref, dq_low, dk_total, dv_total, delta_ref,
):
    count = q_ref.shape[0]
    end_one, end_two = ends_ref[0], ends_ref[1]
    pair = pl.program_id(0)

    @pl.when(pair == 0)
    def _():
        build_bias(bias_ref, valid_ref, end_one, end_two)

    dk_total[...] = jnp.zeros_like(dk_total)
    dv_total[...] = jnp.zeros_like(dv_total)
    product = (do_ref[...].astype(f32) * ctx_ref[...].astype(f32)).T
    for member in range(2):
        rows = product[member * HEAD : (member + 1) * HEAD]
        delta_ref[member : member + 1, :] = jnp.sum(rows, axis=0, keepdims=True)

    def step(index, carry):
        first_row = pl.multiple_of(index * QUERY_ROWS, QUERY_ROWS)
        queries = pl.ds(first_row, QUERY_ROWS)

        def body(width, start):
            window = pl.ds(start, width)
            keys, value, bias = k_ref[window, :], v_ref[window, :], bias_ref[window, queries]
            query, grad = q_ref[queries, :] * bf16(HEAD**-0.5), do_ref[queries, :]
            d_queries, all_probs, all_scores, all_query, all_grad = [], [], [], [], []
            for member in range(2):
                own_query, own_grad = only(query, member), only(grad, member)
                probs = jnp.exp(dot_cols(keys, own_query) + bias - lse_ref[member, :, queries])
                d_probs = dot_cols(value, own_grad)
                d_scores = (probs * (d_probs - delta_ref[member : member + 1, queries])).astype(bf16)
                all_probs.append(probs.astype(bf16))
                all_scores.append(d_scores)
                all_query.append(own_query)
                all_grad.append(own_grad)
                d_queries.append(dot_rows(keys, d_scores))
            dv_total[window, :] += dot(
                jnp.concatenate(all_probs, axis=1), jnp.concatenate(all_grad, axis=0)
            )
            dk_total[window, :] += dot(
                jnp.concatenate(all_scores, axis=1), jnp.concatenate(all_query, axis=0)
            )
            dq_low[queries, :] = (by_member(*d_queries) * HEAD**-0.5).astype(bf16)

        over_window(first_row, end_one, end_two, count, body, BACK_WIDTHS)
        return carry

    lax.fori_loop(0, count // QUERY_ROWS, step, 0)
    parts = (dq_low[...], dk_total[...].astype(bf16), dv_total[...].astype(bf16))
    for part, low in enumerate(parts):
        at = (part * PAIRS_PER_CHUNK + pair) * LANES
        grad_ref[:, pl.ds(pl.multiple_of(at, LANES), LANES)] = low
        if part != 1:
            sums_ref[part // 2 : part // 2 + 1, :] = jnp.sum(low.astype(f32), axis=0, keepdims=True)


def attention_backward(chunk, qkv, d_ctx, ctx, lse, valid_column, ends):
    count, pairs = qkv.shape[0], PAIRS_PER_CHUNK

    def block(offset):
        return pl.BlockSpec((count, LANES), lambda i, ends: (0, i + offset))

    return pl.pallas_call(
        partial(backward_kernel, chunk),
        grid_spec=pltpu.PrefetchScalarGridSpec(
            num_scalar_prefetch=1,
            grid=(pairs,),
            in_specs=[
                block(0),
                block(pairs),
                block(2 * pairs),
                block(chunk * pairs),
                block(chunk * pairs),
                pl.BlockSpec((2, 1, count), lambda i, ends: (i, 0, 0)),
                pl.BlockSpec((count, 1), lambda i, ends: (0, 0)),
            ],
            out_specs=[
                pl.BlockSpec(qkv.shape, lambda i, ends: (0, 0)),
                pl.BlockSpec((8, LANES), lambda i, ends: (0, i)),
            ],
            scratch_shapes=[
                pltpu.VMEM((count, count), f32),
                pltpu.VMEM((count, LANES), bf16),
                pltpu.VMEM((count, LANES), f32),
                pltpu.VMEM((count, LANES), f32),
                pltpu.VMEM((8, count), f32),
            ],
        ),
        out_shape=[
            jax.ShapeDtypeStruct(qkv.shape, bf16),
            jax.ShapeDtypeStruct((8, pairs * LANES), f32),
        ],
        compiler_params=pltpu.CompilerParams(vmem_limit_bytes=VMEM_BYTES),
        cost_estimate=BRIEF,
        name="attention_backward",
    )(ends, qkv, qkv, qkv, d_ctx, ctx, lse, valid_column)


def bits(size):
    return [1 << k for k in reversed(range(size.bit_length() - 1))]


def add_low(left, right):
    return (left.astype(f32) + right.astype(f32)).astype(bf16)


def hold(*values):
    return lax.optimization_barrier(values)


def hold(*values):
    return lax.optimization_barrier(values)


class Fabric:
    def __init__(self):
        self.dp, self.unit = lax.axis_size("dp"), lax.axis_size("unit")
        self.size = self.dp * self.unit
        self.at_unit = lax.axis_index("unit")
        self.at_dp = lax.axis_index("dp")
        self.me = self.at_dp * self.unit + self.at_unit
        dp_bits, unit_bits = [bit * self.unit for bit in bits(self.dp)], bits(self.unit)
        self.top, self.near, self.far, self.core = dp_bits[:-1], dp_bits[-1], unit_bits[:-1], unit_bits[-1]
        self.offsets = [0]
        for bit in self.far:
            self.offsets = self.offsets + [u ^ bit for u in self.offsets]

    def swap(self, value, bit):
        return lax.ppermute(value, AXES, [(i, i ^ bit) for i in range(self.size)])

    def assemble(self, block, places):
        flat = jnp.stack(places).astype(jnp.int32)

        def kernel(place_ref, source, out):
            for row in range(source.shape[0]):
                out[place_ref[row]] = source[row]

        whole = pl.BlockSpec(memory_space=pltpu.VMEM)
        out = pl.pallas_call(
            kernel,
            in_specs=[pl.BlockSpec(memory_space=pltpu.SMEM), whole],
            out_specs=whole,
            out_shape=jax.ShapeDtypeStruct(block.shape, block.dtype),
            compiler_params=pltpu.CompilerParams(vmem_limit_bytes=16 * 2**20),
            name="assemble",
        )(flat, block)
        return out.reshape(-1, block.shape[2])

    def by_device(self, block, masks):
        return self.assemble(block, [self.me ^ mask for mask in masks])

    def split(self, value, bit, left):
        own = bit if bit in left else -bit
        lower = 1 << (len(left) - 1 - left.index(own))
        value = value.reshape(value.shape[0] // (2 * lower), 2, lower, *value.shape[1:])
        mine = (self.me // bit) % 2 if own > 0 else 0
        out = []
        for choice in (1 - mine, mine):
            half = lax.dynamic_index_in_dim(value, choice, 1, keepdims=False)
            out.append(half.reshape(-1, *half.shape[2:]))
        return tuple(out)

    def total(self, value):
        for bit in bits(self.size)[::-1]:
            value = value + self.swap(value, bit)
        return value


def doubled(fabric, block, masks, bit):
    return jnp.concatenate([block, fabric.swap(block, bit)]), masks + [mask ^ bit for mask in masks]


class Scatter:
    def __init__(self, fabric, send, keep, steps, left):
        self.fabric, self.send, self.keep, self.steps = fabric, send, keep, list(steps)
        self.left = [r for r in left if abs(r) != steps[0]]

    @classmethod
    def of(cls, fabric, grad, steps, left):
        return cls(fabric, *fabric.split(grad, steps[0], left), steps, left)

    def start(self):
        self.other = self.fabric.swap(self.send, self.steps.pop(0))

    def finish(self):
        if not self.steps:
            self.result = (self.keep.astype(f32) + self.other.astype(f32))[0]
            return
        bit = self.steps[0]
        mine, theirs = (self.fabric.split(v, bit, self.left) for v in (self.keep, self.other))
        self.left = [r for r in self.left if abs(r) != bit]
        self.send, self.keep = (
            (a.astype(f32) + b.astype(f32)).astype(bf16) for a, b in zip(mine, theirs)
        )

    @classmethod
    def merge(cls, chains):
        first = chains[0]
        send, keep = (
            jnp.concatenate([getattr(c, name) for c in chains], axis=-1) for name in ("send", "keep")
        )
        return cls(first.fabric, send, keep, first.steps, first.left + first.steps[:1])


def beside(chains, compute):
    for chain in chains:
        chain.start()
    values, others = hold(compute(), [chain.other for chain in chains])
    for chain, other in zip(chains, others):
        chain.other = other
        chain.finish()
    return values


ROWS = 256


def row_call(kernel, count, blocks, constants, outs, sums, scratch, name):
    steps = count // ROWS

    def by_row(a):
        return pl.BlockSpec((ROWS, a.shape[1]), lambda i: (i, 0))

    def whole(a):
        return pl.BlockSpec(a.shape, lambda i: (0,) * len(a.shape))

    return pl.pallas_call(
        partial(kernel, steps),
        grid=(steps,),
        in_specs=[by_row(a) for a in blocks] + [whole(a) for a in constants],
        out_specs=[by_row(a) for a in outs] + [whole(a) for a in sums],
        out_shape=list(outs) + list(sums),
        scratch_shapes=scratch,
        compiler_params=pltpu.CompilerParams(vmem_limit_bytes=VMEM_BYTES),
        cost_estimate=BRIEF,
        name=name,
    )(*blocks, *constants)


def column_sums(value):
    return jnp.sum(value, axis=0, keepdims=True)


def normalize(value):
    mean = jnp.mean(value, axis=-1, keepdims=True)
    centred = value - mean
    root = lax.rsqrt(jnp.mean(centred * centred, axis=-1, keepdims=True) + EPS_NORM)
    return centred * root, root


def normalize_back(grad, hat, root, gain):
    scaled = grad * gain
    mean_one = jnp.mean(scaled, axis=-1, keepdims=True)
    mean_two = jnp.mean(scaled * hat, axis=-1, keepdims=True)
    return root * (scaled - mean_one - hat * mean_two)


def attention_out_kernel(steps, ctx, x, w_out, vec, gate, hat_out, root_out, low_out):
    attn = (dot(ctx[...], w_out[...]) + vec[2:3, :]) * gate[...]
    hat, root = normalize(x[...].astype(f32) + attn)
    hat_out[...] = hat
    root_out[...] = root
    low_out[...] = (hat * vec[3:4, :] + vec[4:5, :]).astype(bf16)


def head_kernel(
    steps, branch, hat_one, teacher, cotangent, valid, w_dist, vec, gate,
    low_out, d_second_out, d_branch_out, sums, g_dist, total,
):
    step = pl.program_id(0)

    @pl.when(step == 0)
    def _():
        sums[...] = jnp.zeros_like(sums)
        total[...] = jnp.zeros_like(total)

    keep = (valid[...] > 0).astype(f32)
    first = hat_one[...] * vec[3:4, :] + vec[4:5, :]
    hat, root = normalize(first + (branch[...] + vec[5:6, :]) * gate[...])
    low = (hat * vec[6:7, :] + vec[7:8, :]).astype(bf16)
    low_out[...] = low
    error = dot(low, w_dist[...]) + vec[8:9, :] - teacher[...].astype(f32)
    kept = keep * error
    d_student = kept.astype(bf16)
    d_out = cotangent[...].astype(f32) + dot_cols(d_student, w_dist[...])
    d_second = normalize_back(d_out, hat, root, vec[6:7, :])
    d_second_out[...] = d_second
    d_branch = (d_second * gate[...]).astype(bf16)
    d_branch_out[...] = d_branch
    sums[0:1, :] += column_sums(d_student.astype(f32))
    sums[1:2, :] += column_sums(d_out * hat)
    sums[2:3, :] += column_sums(d_out)
    sums[3:4, :] += column_sums(d_branch.astype(f32))
    sums[4:5, :] += column_sums(kept * error)
    total[...] += dot_rows(low, d_student)

    @pl.when(step == steps - 1)
    def _():
        g_dist[...] = total[...].astype(bf16)


def attention_out_back_kernel(
    steps, d_first, hat_one, root_one, ctx, w_out, vec, gate, head_gate,
    d_sum_out, d_ctx_out, sums, g_out, total,
):
    step = pl.program_id(0)

    @pl.when(step == 0)
    def _():
        sums[...] = jnp.zeros_like(sums)
        total[...] = jnp.zeros_like(total)

    hat, grad = hat_one[...], d_first[...]
    d_sum = normalize_back(grad, hat, root_one[...], vec[3:4, :])
    d_sum_out[...] = d_sum
    d_attn = (d_sum * gate[...]).astype(bf16)
    d_ctx_out[...] = (dot_cols(d_attn, w_out[...]) * head_gate[...]).astype(bf16)
    sums[0:1, :] += column_sums(d_attn.astype(f32))
    sums[1:2, :] += column_sums(grad * hat)
    sums[2:3, :] += column_sums(grad)
    total[...] += dot_rows(ctx[...], d_attn)

    @pl.when(step == steps - 1)
    def _():
        g_out[...] = total[...].astype(bf16)


def input_grad_kernel(steps, before, d_qkv, weight, out):
    out[...] = before[...] + dot_cols(d_qkv[...], weight[...])


def adamw(master, first, second, grad, rate, decay):
    first_new = BETA_ONE * first + (1.0 - BETA_ONE) * grad
    second_new = BETA_TWO * second + (1.0 - BETA_TWO) * grad * grad
    first_hat = first_new / (1.0 - BETA_ONE**STEP)
    second_hat = second_new / (1.0 - BETA_TWO**STEP)
    master_new = master - rate * (first_hat / (jnp.sqrt(second_hat) + ADAM_EPS) + decay * master)
    return master_new, first_new, second_new


def shards(
    layer_input, teacher, cotangent, key_valid, seg_lengths, head_mask, hidden_mask, inter_mask,
    proj_master, proj_first, proj_second, up_master, up_first, up_second,
    down_master, down_first, down_second, vector_master, vector_first, vector_second,
):
    fabric = Fabric()
    top, near, far, core = fabric.top, fabric.near, fabric.far, fabric.core
    all_bits = top + [near] + far + [core]
    rows, width = layer_input.shape
    span = PAIRS_PER_CHUNK * LANES
    chunks = width // span
    hidden_gate = hidden_mask.astype(f32)[None]
    valid_column = key_valid[:, None]
    ends = jnp.cumsum(seg_lengths[0])
    head_gate = jnp.repeat(head_mask.astype(f32), HEAD)[None]
    vec = vector_master
    tile_rows, units = up_master.shape

    offsets = fabric.offsets + [u ^ core for u in fabric.offsets]

    def by_offset(values, order):
        return [lax.dynamic_index_in_dim(values, fabric.at_unit ^ u, 0, keepdims=False) for u in order]

    inner_bias = by_offset(vec[9:].reshape(fabric.unit, units), offsets)
    unit_gate = by_offset(inter_mask.astype(f32).reshape(fabric.unit, units), offsets)

    def by_chunk(matrix):
        return [
            matrix[..., p * width + c * span : p * width + (c + 1) * span]
            for c in range(chunks)
            for p in range(3)
        ]

    proj_low = proj_master.astype(bf16)
    block, masks = jnp.concatenate(by_chunk(proj_low), axis=1)[None], [0]
    for bit in top:
        block, masks = doubled(fabric, block, masks, bit)
    ones, ones_masks, twos, twos_masks = block[..., : 3 * span], masks, block[..., 3 * span :], masks
    for bit in [near] + far + [core]:
        ones, ones_masks = doubled(fabric, ones, ones_masks, bit)
    for bit in far + [near]:
        twos, twos_masks = doubled(fabric, twos, twos_masks, bit)
    w_qkv = [fabric.by_device(ones, ones_masks)]

    rest = jnp.concatenate(
        [
            up_master.astype(bf16),
            down_master.astype(bf16).T,
            proj_low[:, 3 * width : 4 * width].reshape(-1, units),
            proj_low[:, 4 * width :].reshape(-1, units),
        ]
    )
    rest = lax.all_gather(rest, AXES, axis=0).reshape(fabric.dp, fabric.unit, -1, units)
    count = (rest.shape[2] - 2 * tile_rows) // 2

    def tile(u, at):
        size = (fabric.dp, 1, tile_rows, units)
        return lax.dynamic_slice(rest, (0, fabric.at_unit ^ u, at, 0), size).reshape(width, units)

    w_up, w_down = ([tile(u, at) for u in offsets] for at in (0, tile_rows))
    w_out, w_dist = (
        rest[:, :, at : at + count].reshape(width, width)
        for at in (2 * tile_rows, 2 * tile_rows + count)
    )

    bias_qkv = jnp.concatenate(
        by_chunk(jnp.concatenate([vec[0], jnp.zeros_like(vec[0]), vec[1]]))
    ).reshape(chunks, 3 * span)

    def project(c):
        return (dot(layer_input, w_qkv[c]) + bias_qkv[c]).astype(bf16)

    qkv, lse, ctx = [project(0)], [], None

    def attend(ctx):
        c = len(lse)
        ctx, part = attention_forward(c, qkv[c], valid_column, ends, head_mask, ctx, width)
        lse.append(part)
        return ctx

    qkv[0], twos = hold(qkv[0], twos)
    other = fabric.swap(twos, core)
    ctx, other = hold(attend(ctx), other)
    late = fabric.by_device(
        jnp.concatenate([twos, other]), twos_masks + [mask ^ core for mask in twos_masks]
    )
    w_qkv += [late[:, c * 3 * span : (c + 1) * 3 * span] for c in range(chunks - 1)]
    for c in range(1, chunks):
        qkv.append(project(c))
        ctx = attend(ctx)

    def like(kind, *shape):
        return jax.ShapeDtypeStruct(shape or (rows, width), kind)

    hat_one, root_one, first_low = row_call(
        attention_out_kernel, rows, [ctx, layer_input], [w_out, vec, hidden_gate],
        [like(f32), like(f32, rows, 1), like(bf16)], [], [], "attention_out",
    )
    branch, active, slope = 0.0, [], []
    for u in range(fabric.unit):
        inner = dot(first_low, w_up[u]) + inner_bias[u]
        cdf = 0.5 * (1.0 + lax.erf(inner * 0.7071067811865476))
        pdf = jnp.exp(-0.5 * inner * inner) * 0.3989422804014327
        active.append((inner * cdf * unit_gate[u]).astype(bf16))
        slope.append((cdf + inner * pdf) * unit_gate[u])
        branch = branch + dot_cols(active[u], w_down[u])
    out_low, d_second, d_branch, head_sums, g_dist = row_call(
        head_kernel, rows, [branch, hat_one, teacher, cotangent, valid_column],
        [w_dist, vec, hidden_gate], [like(bf16), like(f32), like(bf16)],
        [like(f32, 8, width), like(bf16, width, width)],
        [pltpu.VMEM((width, width), f32)], "head",
    )

    unit_bits, dp_bits = far + [core], top + [near]
    blocks = len(fabric.offsets)
    block_bits = [-bit for bit in far[::-1]] + dp_bits

    def stacked(grads):
        return jnp.stack(grads).reshape(blocks * fabric.dp, tile_rows, units)

    def g_blocks(make):
        return [stacked([make(u) for u in side]) for side in (range(blocks, 2 * blocks), range(blocks))]

    g_down = g_blocks(lambda u: dot_rows(d_branch, active[u]).astype(bf16))
    r_down = Scatter(fabric, *g_down, [core, near] + far[::-1] + top[::-1], [core] + block_bits)
    r_down.start()
    d_inner = [(dot(d_branch, w_down[u]) * slope[u]).astype(bf16) for u in range(2 * blocks)]
    g_up = g_blocks(lambda u: dot_rows(first_low, d_inner[u]).astype(bf16))
    g_inner_bias = [jnp.sum(d.astype(f32), axis=0) for d in d_inner]
    *g_up, r_down.other = hold(*g_up, r_down.other)
    r_down.finish()
    r_up = Scatter(fabric, *g_up, [core] + far[::-1] + [near] + top[::-1], [core] + block_bits)
    order = [core] + far[::-1] + [near] + top[::-1]

    def feed_forward_back():
        return sum((dot_cols(d_inner[u], w_up[u]) for u in range(2 * blocks)), d_second)

    def attention_out_back():
        return row_call(
            attention_out_back_kernel, rows, [d_first, hat_one, root_one, ctx],
            [w_out, vec, hidden_gate, head_gate], [like(f32), like(bf16)],
            [like(f32, 8, width), like(bf16, width, width)],
            [pltpu.VMEM((width, width), f32)], "attention_out_back",
        )

    def attend_back(c):
        return attention_backward(c, qkv[c], d_ctx, ctx, lse[c], valid_column, ends)

    def add_input_grad(c):
        if c >= chunks:
            return [input_grad]
        return row_call(
            input_grad_kernel, rows, [input_grad, d_qkv[c]], [w_qkv[c]], [like(f32)], [], [], "input_grad"
        )

    def scatter(grad):
        grad = grad.reshape(fabric.size, -1, grad.shape[1])
        return Scatter.of(fabric, grad, order, dp_bits + unit_bits)

    r_down.start()
    d_first = beside([r_up], feed_forward_back)
    d_qkv, bias_sums, chains = [], [], []
    for c in range(chunks):
        if c == 0:

            def compute():
                global_parts = attention_out_back()
                return global_parts, attention_backward(
                    0, qkv[0], global_parts[1], ctx, lse[0], valid_column, ends
                )

            r_up.start()
            (d_first_sum, d_ctx, out_sums, g_out), (grad, sums) = compute()
            grad, d_ctx, r_up.other, r_down.other = hold(grad, d_ctx, r_up.other, r_down.other)
            r_up.finish()
            r_down.finish()
            rings = [r_up, r_down]
        else:
            while len(rings[0].steps) > len(top) + 1:
                beside(rings, lambda: 0)
            grad, sums = beside(rings + chains, lambda: attend_back(c))
            if len(rings) > 1 and len(rings[0].steps) == len(top):
                rings = [Scatter.merge(rings)]
        d_qkv.append(grad)
        bias_sums.append(sums[:2])
        mine = dot_rows(layer_input, grad).astype(bf16)
        if c == 0:
            mine = jnp.concatenate([mine, g_out, g_dist], axis=1)
        chains.append(scatter(mine))
    input_grad, c = d_first_sum, 0
    while len(chains[-1].steps) > len(top):
        busy = [chain for chain in rings + chains if chain.steps]
        (input_grad,) = beside(busy, lambda: add_input_grad(c))
        c += 1
    while c < chunks:
        (input_grad,) = add_input_grad(c)
        c += 1
    late = [chain for chain in chains if len(chain.steps) == len(top)]
    done = [chain for chain in chains if len(chain.steps) < len(top)]
    last = Scatter.merge(late)
    while last.steps:
        beside([chain for chain in rings + [last] + done if chain.steps], lambda: 0)
    results, at = [chain.result for chain in done], 0
    for chain in late:
        size = chain.keep.shape[-1]
        results.append(last.result[:, at : at + size])
        at += size
    g_proj = jnp.concatenate(
        [result[:, p * span : (p + 1) * span] for p in range(3) for result in results]
        + [results[0][:, 3 * span :]],
        axis=1,
    )
    g_up, g_down = rings[0].result[:, :units], rings[0].result[:, units:]
    g_inner_bias = dict(zip(offsets, g_inner_bias))
    g_inner_bias = by_offset(jnp.stack([g_inner_bias[u] for u in range(fabric.unit)]), range(fabric.unit))

    squares = sum(jnp.sum(g * g) for g in (g_proj, g_up, g_down))
    table = jnp.concatenate(
        [
            jnp.concatenate(bias_sums, axis=1),
            out_sums[:3],
            head_sums[3:4],
            head_sums[1:3],
            head_sums[:1],
            jnp.stack(g_inner_bias).reshape(-1, width),
            head_sums[4:5],
            jnp.full((1, width), squares),
        ]
    )
    table = fabric.total(table)
    vector_grad, error_total, square_total = table[:-2], jnp.sum(table[-2]), table[-1, 0]
    grad_norm = jnp.sqrt(square_total + jnp.sum(vector_grad * vector_grad))
    clip = jnp.minimum(1.0, CLIP_NORM / (grad_norm + 1e-06))
    distill_loss = error_total / (rows * fabric.size * width)
    return (
        out_low,
        input_grad,
        grad_norm,
        distill_loss,
        *adamw(proj_master, proj_first, proj_second, clip * g_proj, RATE_MATRIX, DECAY_MATRIX),
        *adamw(up_master, up_first, up_second, clip * g_up, RATE_MATRIX, DECAY_MATRIX),
        *adamw(down_master, down_first, down_second, clip * g_down.T, RATE_MATRIX, DECAY_MATRIX),
        *adamw(vector_master, vector_first, vector_second, clip * vector_grad, RATE_VECTOR, 0.0),
    )


def solution(mesh):
    by_token = P(AXES, None)
    tile, tile_back = P("dp", "unit"), P("unit", "dp")
    in_specs = (
        (by_token, by_token, by_token, P(AXES), by_token, P(), P(), P())
        + (by_token,) * 3
        + (tile,) * 3
        + (tile_back,) * 3
        + (P(),) * 3
    )
    out_specs = (
        (by_token, by_token, P(), P()) + (by_token,) * 3 + (tile,) * 3 + (tile_back,) * 3 + (P(),) * 3
    )
    return jax.shard_map(shards, mesh=mesh, in_specs=in_specs, out_specs=out_specs, check_vma=False)
```
